32 devices in a mesh: tp: 2 (over y), cp: 16 (over z, x, core).
Axes of the slice: x: 2, y: 2, z: 4, core: 2. Of those that a mesh axis runs over, the one named last changes fastest.
Arguments:
- features: bfloat16 [3, 2176, 8192], P(None, 'cp', 'tp'), may hold values from -6 to 6
- short_filter: float32 [3, 3, 8192], P(None, None, 'tp'), may hold values from -4 to 4
- long_filter: float32 [128, 8192], P(None, 'tp'), may hold values from -0.5 to 0.5
- skip_scale: float32 [8192], P('tp'), may hold values from -4 to 4
- out_weight: bfloat16 [8192, 8192], P('tp', 'cp'), may hold values from -0.09375 to 0.09375
Outputs:
- mixed: bfloat16 [2176, 8192], P('cp', 'tp')
The draws below stay inside these ranges and needn't reach their ends.
All inputs are finite; a program needn't handle non-finite values.
Results may differ from the reference program's by a relative error of at most 0.017.
Values may be sent and summed in bfloat16 or wider, within the bound.
A program may use at most 192 MiB of HBM per device.

```python
import jax
import jax.numpy as jnp
from jax import lax

D = 8192
C = 8192
TAPS = 128
SHORT = 3
TOKENS = 2176
N_TP = 2


def spiked(array, rng, source, target, shards_of, factor):
    def block_of(dim):
        return (jnp.arange(array.shape[dim]) // (array.shape[dim] // shards_of)).reshape((-1,) + (1,) * (array.ndim - 1 - dim))

    first = jax.random.permutation(rng, shards_of)[block_of(target)]
    far = (block_of(target) + shards_of // 2) % shards_of
    return jnp.where((block_of(source) == first) | (block_of(source) == far), factor * array, array)


def levels(stream_key, dims, split, least, high):
    def one(dim, parts):
        steps = jax.random.uniform(jax.random.fold_in(jax.random.fold_in(stream_key, 6), dim), (parts,), jnp.float32, least / len(split), high / len(split))
        return jnp.repeat(jnp.exp(steps), dims[dim] // parts).reshape((-1,) + (1,) * (len(dims) - dim - 1))

    loudness = one(*split[0])
    for cut in split[1:]:
        loudness = loudness * one(*cut)
    return loudness


def bell_draw(stream_key, shape, spread, reach, split=(), kind=jnp.bfloat16):
    result = spread * jax.random.normal(stream_key, shape, jnp.float32)
    if split:
        result = result * levels(stream_key, shape, split, -0.22, 0.18)
    return jnp.clip(result, -reach, reach).astype(kind)


def bell_draw_with(own_key, dims, deviation, reach, split, heavy, kind=jnp.bfloat16):
    drawn = deviation * jax.random.normal(own_key, dims, jnp.float32)
    if split:
        drawn = drawn * levels(own_key, dims, split, -0.22, 0.18)
    return jnp.clip(spiked(drawn, jax.random.fold_in(own_key, 3), *heavy), -reach, reach).astype(kind)


def setup_inputs(seed: int = 0) -> dict:
    key_list = jax.random.split(jax.random.key(seed), 6)
    return {
        "features": bell_draw(key_list[0], (3, TOKENS, C), 1.0, 6.0, ((1, 16), (2, 2))),
        "short_filter": bell_draw(key_list[1], (3, SHORT, C), 0.6, 4.0, ((2, 2),), jnp.float32),
        "long_filter": bell_draw(key_list[2], (TAPS, C), TAPS ** -0.5, 0.5, ((1, 2),), jnp.float32),
        "skip_scale": bell_draw(key_list[3], (C,), 1.0, 4.0, ((0, 2),), jnp.float32),
        "out_weight": bell_draw_with(key_list[4], (C, D), C ** -0.5, 0.09375, ((0, 2), (1, 16)), (0, 1, 16, 2.0)),
    }


def short_conv(extended, short_filter):
    out_rows = extended.shape[1] - (SHORT - 1)
    summed = jnp.zeros((extended.shape[0], out_rows, extended.shape[2]), jnp.float32)
    for lag in range(SHORT):
        begin = SHORT - 1 - lag
        summed = summed + short_filter[:, lag, None, :] * extended[:, begin:begin + out_rows, :]
    return summed


def long_conv(product_ext, long_filter, skip_scale):
    out_rows = product_ext.shape[0] - (TAPS - 1)
    summed = skip_scale[None, :] * product_ext[TAPS - 1:]
    for lag in range(TAPS):
        begin = TAPS - 1 - lag
        summed = summed + long_filter[lag][None, :] * product_ext[begin:begin + out_rows]
    return summed


def reference(features, short_filter, long_filter, skip_scale, out_weight):
    channels = C // N_TP

    def one_group(summed, group_index):
        offset = group_index * channels
        inputs_block = lax.dynamic_slice_in_dim(features, offset, channels, 2).astype(jnp.float32)
        filter_block = lax.dynamic_slice_in_dim(short_filter, offset, channels, 2)
        long_block = lax.dynamic_slice_in_dim(long_filter, offset, channels, 1)
        skip_block = lax.dynamic_slice_in_dim(skip_scale, offset, channels, 0)
        weights = lax.dynamic_slice_in_dim(out_weight, offset, channels, 0)
        extended = jnp.pad(inputs_block, ((0, 0), (SHORT - 1, 0), (0, 0)))
        shorted = short_conv(extended, filter_block)
        product = shorted[1] * shorted[2]
        product_ext = jnp.pad(product, ((TAPS - 1, 0), (0, 0)))
        filtered = long_conv(product_ext, long_block, skip_block)
        gated = (shorted[0] * filtered).astype(jnp.bfloat16)
        partial_value = jnp.dot(gated, weights, preferred_element_type=jnp.float32).astype(jnp.bfloat16)
        partial_value = lax.optimization_barrier(partial_value).astype(jnp.float32)
        return summed + partial_value, None

    summed, _ = lax.scan(one_group, jnp.zeros((TOKENS, D), jnp.float32), jnp.arange(N_TP, dtype=jnp.int32))
    return summed.astype(jnp.bfloat16)
```

```python
import functools

import jax
import jax.numpy as jnp
from jax import lax
from jax.experimental import pallas as pl
from jax.experimental.pallas import tpu as pltpu
from jax.sharding import PartitionSpec as P

TAPS = 128
SHORT = 3
LANES = 128
SUB = 8


def from_behind(block, axis, distance):
    devices = range(lax.axis_size(axis))
    route = [(i - distance, i) for i in devices if i - distance in devices]
    return lax.ppermute(block, axis, route)


def conv_kernel(rows, width, feat_ref, halo_ref, edge_ref, short_ref, long_ref, skip_ref, out_ref, ext, prod):
    def strip(index, carry):
        lanes = pl.ds(pl.multiple_of(index * LANES, LANES), LANES)
        shorted = []
        for i in range(3):
            ext[i, pl.ds(0, SUB), :] = edge_ref[i, :, lanes].astype(jnp.float32)
            ext[i, pl.ds(SUB, rows), :] = feat_ref[i, :, lanes].astype(jnp.float32)
            total = short_ref[i, pl.ds(0, 1), lanes] * ext[i, pl.ds(SUB, rows), :]
            for lag in range(1, SHORT):
                total = total + short_ref[i, pl.ds(lag, 1), lanes] * ext[i, pl.ds(SUB - lag, rows), :]
            shorted.append(total)
        product = shorted[1] * shorted[2]
        prod[pl.ds(0, TAPS), :] = halo_ref[:, lanes].astype(jnp.float32)
        prod[pl.ds(TAPS, rows), :] = product
        total = skip_ref[:, lanes] * product
        span = rows + TAPS - SUB
        for r in range(SUB):
            shifted = prod[pl.ds(SUB - r, span), :]
            for m in range(TAPS // SUB):
                begin = TAPS - SUB - SUB * m
                total = total + long_ref[pl.ds(SUB * m + r, 1), lanes] * shifted[begin:begin + rows]
        out_ref[:, lanes] = (shorted[0] * total).astype(jnp.bfloat16)
        return carry

    lax.fori_loop(0, width // LANES, strip, 0)


def gate_conv(features, halo, edge, short_filter, long_filter, skip_scale):
    _, rows, channels = features.shape
    width = min(512, channels)
    return pl.pallas_call(
        functools.partial(conv_kernel, rows, width),
        grid=(channels // width,),
        out_shape=jax.ShapeDtypeStruct((rows, channels), jnp.bfloat16),
        in_specs=[
            pl.BlockSpec((3, rows, width), lambda c: (0, 0, c)),
            pl.BlockSpec((TAPS, width), lambda c: (0, c)),
            pl.BlockSpec((3, SUB, width), lambda c: (0, 0, c)),
            pl.BlockSpec((3, SHORT, width), lambda c: (0, 0, c)),
            pl.BlockSpec((TAPS, width), lambda c: (0, c)),
            pl.BlockSpec((1, width), lambda c: (0, c)),
        ],
        out_specs=pl.BlockSpec((rows, width), lambda c: (0, c)),
        scratch_shapes=[
            pltpu.VMEM((3, SUB + rows, LANES), jnp.float32),
            pltpu.VMEM((TAPS + rows, LANES), jnp.float32),
        ],
        compiler_params=pltpu.CompilerParams(vmem_limit_bytes=32 * 2**20),
        cost_estimate=pl.CostEstimate(
            flops=2 * TAPS * rows * channels, bytes_accessed=10 * rows * channels, transcendentals=0
        ),
        name="gate_conv",
    )(features, halo, edge, short_filter, long_filter, skip_scale.reshape(1, channels))


def halo_of(features, short_filter):
    rows = features.shape[1]
    tail = features[1:, rows - TAPS - SHORT + 1:, :].astype(jnp.float32)
    shorted = sum(
        short_filter[1:, lag, None, :] * tail[:, SHORT - 1 - lag:SHORT - 1 - lag + TAPS] for lag in range(SHORT)
    )
    product = (shorted[0] * shorted[1]).astype(jnp.bfloat16)
    return product, features[:, rows - SUB:, :]


def local(features, short_filter, long_filter, skip_scale, out_weight):
    product, edge = halo_of(features, short_filter)
    halo = from_behind(product, "cp", 1)
    edge = from_behind(edge, "cp", 1)
    gated = gate_conv(features, halo, edge, short_filter, long_filter, skip_scale)
    everyone = lax.all_gather(gated, "cp", axis=0, tiled=True)
    partial_value = jnp.dot(everyone, out_weight, preferred_element_type=jnp.float32).astype(jnp.bfloat16)
    mine = lax.all_to_all(partial_value, "cp", split_axis=0, concat_axis=1, tiled=True)
    return lax.psum_scatter(mine, "tp", scatter_dimension=1, tiled=True)


def solution(mesh):
    return jax.shard_map(
        local,
        mesh=mesh,
        in_specs=(P(None, "cp", "tp"), P(None, None, "tp"), P(None, "tp"), P("tp"), P("tp", "cp")),
        out_specs=P("cp", "tp"),
        check_vma=False,
    )
```

```python
import functools

import jax
import jax.numpy as jnp
from jax import lax
from jax.experimental import pallas as pl
from jax.experimental.pallas import tpu as pltpu
from jax.sharding import PartitionSpec as P

TAPS = 128
SHORT = 3
LANES = 128
SUB = 8


def from_behind(block, axis, distance):
    devices = range(lax.axis_size(axis))
    route = [(i - distance, i) for i in devices if i - distance in devices]
    return lax.ppermute(block, axis, route)


def conv_kernel(rows, width, feat_ref, halo_ref, edge_ref, short_ref, long_ref, skip_ref, out_ref, ext, prod):
    def strip(index, carry):
        lanes = pl.ds(pl.multiple_of(index * LANES, LANES), LANES)
        shorted = []
        for i in range(3):
            ext[i, pl.ds(0, SUB), :] = edge_ref[i, :, lanes].astype(jnp.float32)
            ext[i, pl.ds(SUB, rows), :] = feat_ref[i, :, lanes].astype(jnp.float32)
            total = short_ref[i, pl.ds(0, 1), lanes] * ext[i, pl.ds(SUB, rows), :]
            for lag in range(1, SHORT):
                total = total + short_ref[i, pl.ds(lag, 1), lanes] * ext[i, pl.ds(SUB - lag, rows), :]
            shorted.append(total)
        product = shorted[1] * shorted[2]
        prod[pl.ds(0, TAPS), :] = halo_ref[:, lanes].astype(jnp.float32)
        prod[pl.ds(TAPS, rows), :] = product
        total = skip_ref[:, lanes] * product
        span = rows + TAPS - SUB
        for r in range(SUB):
            shifted = prod[pl.ds(SUB - r, span), :]
            for m in range(TAPS // SUB):
                begin = TAPS - SUB - SUB * m
                total = total + long_ref[pl.ds(SUB * m + r, 1), lanes] * shifted[begin:begin + rows]
        out_ref[pl.ds(0, rows), lanes] = (shorted[0] * total).astype(jnp.bfloat16)
        if out_ref.shape[0] > rows:
            out_ref[pl.ds(rows, out_ref.shape[0] - rows), lanes] = jnp.zeros(
                (out_ref.shape[0] - rows, LANES), jnp.bfloat16
            )
        return carry

    lax.fori_loop(0, width // LANES, strip, 0)


def gate_conv(features, halo, edge, short_filter, long_filter, skip_scale, out_rows):
    _, rows, channels = features.shape
    width = min(512, channels)
    return pl.pallas_call(
        functools.partial(conv_kernel, rows, width),
        grid=(channels // width,),
        out_shape=jax.ShapeDtypeStruct((out_rows, channels), jnp.bfloat16),
        in_specs=[
            pl.BlockSpec((3, rows, width), lambda c: (0, 0, c)),
            pl.BlockSpec((TAPS, width), lambda c: (0, c)),
            pl.BlockSpec((3, SUB, width), lambda c: (0, 0, c)),
            pl.BlockSpec((3, SHORT, width), lambda c: (0, 0, c)),
            pl.BlockSpec((TAPS, width), lambda c: (0, c)),
            pl.BlockSpec((1, width), lambda c: (0, c)),
        ],
        out_specs=pl.BlockSpec((out_rows, width), lambda c: (0, c)),
        scratch_shapes=[
            pltpu.VMEM((3, SUB + rows, LANES), jnp.float32),
            pltpu.VMEM((TAPS + rows, LANES), jnp.float32),
        ],
        compiler_params=pltpu.CompilerParams(vmem_limit_bytes=32 * 2**20),
        cost_estimate=pl.CostEstimate(
            flops=2 * TAPS * rows * channels, bytes_accessed=10 * rows * channels, transcendentals=0
        ),
        name="gate_conv",
    )(features, halo, edge, short_filter, long_filter, skip_scale.reshape(1, channels))


def halo_of(features, short_filter):
    rows = features.shape[1]
    tail = features[1:, rows - TAPS - SHORT + 1:, :].astype(jnp.float32)
    shorted = sum(
        short_filter[1:, lag, None, :] * tail[:, SHORT - 1 - lag:SHORT - 1 - lag + TAPS] for lag in range(SHORT)
    )
    product = (shorted[0] * shorted[1]).astype(jnp.bfloat16)
    return product, features[:, rows - SUB:, :]


def ring_kernel(
    n, rows, gated_ref, weight_ref, out_ref, blocks, weights, kept, sent, other, summed, landed,
    own_sem, block_send, block_recv, weight_send, weight_recv, tp_send, tp_recv, out_send, out_recv,
):
    t, cp = lax.axis_index("tp"), lax.axis_index("cp")
    core, chip = cp % 2, cp // 2
    x, z = chip % 2, chip // 2
    depth = n // 2
    place = x * (n - 1 - z) + (1 - x) * z
    forth = 1 - 2 * core
    half_owner = chip // depth
    my_piece = (chip % depth) * 2 + t

    def cp_at(ring_place):
        r = (ring_place + 2 * n) % n
        rx = r // depth
        rz = rx * (n - 1 - r) + (1 - rx) * r
        return (rz * 2 + rx) * 2 + core

    def peer(a, b):
        return dict(device_id=(a, b), device_id_type=pl.DeviceIdType.MESH)

    ahead, behind = cp_at(place + forth), cp_at(place - forth)
    sibling = cp + 1 - 2 * core

    barrier = pltpu.get_barrier_semaphore()
    for device in ((t, ahead), (t, behind), (t, sibling), (1 - t, cp)):
        pl.semaphore_signal(barrier, inc=1, **peer(*device))

    def greet(i, carry):
        sender = (t * depth + i // 2) * 2 + core

        @pl.when(jnp.logical_or(i % 2 != t, sender != cp))
        def _():
            pl.semaphore_signal(barrier, inc=1, **peer(i % 2, sender))

        return carry

    lax.fori_loop(0, n, greet, 0)
    pl.semaphore_wait(barrier, 4 + n - 1 + (half_owner + t) % 2)

    def send_own(slot, device):
        return pltpu.make_async_remote_copy(
            src_ref=gated_ref, dst_ref=blocks.at[slot], send_sem=block_send.at[slot], recv_sem=block_recv.at[slot],
            **peer(t, device),
        )

    def pass_on(slot):
        odd = slot % 2
        return pltpu.make_async_remote_copy(
            src_ref=blocks.at[slot], dst_ref=blocks.at[slot + 2], send_sem=block_send.at[slot + 2],
            recv_sem=block_recv.at[slot + 2], **peer(t, odd * ahead + (1 - odd) * behind),
        )

    first, second = send_own(1, ahead), send_own(2, behind)
    first.start()
    second.start()
    columns = pltpu.make_async_remote_copy(
        src_ref=weight_ref, dst_ref=weights.at[core], send_sem=weight_send, recv_sem=weight_recv, **peer(t, sibling)
    )
    columns.start()
    own_columns = pltpu.make_async_copy(weight_ref, weights.at[core], own_sem.at[0])
    own_columns.start()
    own_block = pltpu.make_async_copy(gated_ref, blocks.at[0], own_sem.at[1])
    own_block.start()
    own_columns.wait()
    own_block.wait()
    columns.wait_recv()

    def tp_copy(slot):
        return pltpu.make_async_remote_copy(
            src_ref=sent.at[slot], dst_ref=other.at[slot], send_sem=tp_send.at[slot], recv_sem=tp_recv.at[slot],
            **peer(1 - t, cp),
        )

    def out_copy(slot):
        odd, step = slot % 2, (slot + 1) // 2
        return pltpu.make_async_remote_copy(
            src_ref=summed.at[slot], dst_ref=landed.at[my_piece], send_sem=out_send.at[slot],
            recv_sem=out_recv.at[my_piece], **peer(half_owner, cp_at(place + (1 - 2 * odd) * forth * step)),
        )

    tile = min(256, weights.shape[2])

    def multiply(slot, side, target):
        def one(j, carry):
            lanes = pl.ds(pl.multiple_of(j * tile, tile), tile)
            target[slot, :, lanes] = jnp.dot(
                blocks[slot], weights[side, :, lanes], preferred_element_type=jnp.float32
            ).astype(jnp.bfloat16)
            return carry

        lax.fori_loop(0, weights.shape[2] // tile, one, 0)

    def finish(slot):
        tp_copy(slot).wait_recv()
        total = (kept[slot].astype(jnp.float32) + other[slot].astype(jnp.float32)).astype(jnp.bfloat16)
        stays = jnp.logical_and(slot == 0, half_owner == t)

        @pl.when(stays)
        def _():
            landed[my_piece] = total

        @pl.when(jnp.logical_not(stays))
        def _():
            summed[slot] = total
            out_copy(slot).start()

    def step(slot, carry):
        @pl.when(slot > 0)
        def _():
            pltpu.make_async_copy(blocks.at[slot], blocks.at[slot], block_recv.at[slot]).wait()

        @pl.when(jnp.logical_and(slot > 0, slot + 2 < n))
        def _():
            pass_on(slot).start()

        multiply(slot, 1 - t, sent)
        tp_copy(slot).start()
        multiply(slot, t, kept)

        @pl.when(slot > 0)
        def _():
            finish(slot - 1)

        return carry

    lax.fori_loop(0, n, step, 0)
    finish(n - 1)

    first.wait_send()
    second.wait_send()
    columns.wait_send()

    def drain(slot, carry):
        @pl.when(jnp.logical_and(slot > 0, slot + 2 < n))
        def _():
            pass_on(slot).wait_send()

        tp_copy(slot).wait_send()

        @pl.when(jnp.logical_not(jnp.logical_and(slot == 0, half_owner == t)))
        def _():
            out_copy(slot).wait_send()

        return carry

    lax.fori_loop(0, n, drain, 0)
    for piece in range(n):
        @pl.when(jnp.logical_not(jnp.logical_and(piece == my_piece, half_owner == t)))
        def _():
            pltpu.make_async_copy(landed.at[piece], landed.at[piece], out_recv.at[piece]).wait()

        width = landed.shape[2]
        out_ref[:, pl.ds(piece * width, width)] = landed[piece, pl.ds(0, rows), :]


def project(gated, out_weight, rows, n):
    padded, channels = gated.shape
    width = out_weight.shape[1]
    kind = jnp.bfloat16
    dma = pltpu.SemaphoreType.DMA
    return pl.pallas_call(
        functools.partial(ring_kernel, n, rows),
        out_shape=jax.ShapeDtypeStruct((rows, n * width), kind),
        in_specs=[pl.BlockSpec(memory_space=pl.ANY)] * 2,
        out_specs=pl.BlockSpec(memory_space=pltpu.VMEM),
        scratch_shapes=[
            pltpu.VMEM((n, padded, channels), kind),
            pltpu.VMEM((2, channels, width), kind),
            *[pltpu.VMEM((n, padded, width), kind)] * 5,
            dma((2,)), dma((n,)), dma((n,)), dma, dma, dma((n,)), dma((n,)), dma((n,)), dma((n,)),
        ],
        compiler_params=pltpu.CompilerParams(
            collective_id=0, has_side_effects=True, vmem_limit_bytes=48 * 2**20
        ),
        cost_estimate=pl.CostEstimate(
            flops=4 * n * padded * channels * width, bytes_accessed=4 * channels * width, transcendentals=0
        ),
        name="ring_project",
    )(gated, out_weight)


def local(on_ring, features, short_filter, long_filter, skip_scale, out_weight):
    rows = features.shape[1]
    product, edge = halo_of(features, short_filter)
    halo = from_behind(product, "cp", 1)
    edge = from_behind(edge, "cp", 1)
    out_rows = -(-rows // 16) * 16 if on_ring else rows
    gated = gate_conv(features, halo, edge, short_filter, long_filter, skip_scale, out_rows)
    if on_ring:
        return project(gated, out_weight, rows, lax.axis_size("cp") // 2)
    everyone = lax.all_gather(gated, "cp", axis=0, tiled=True)
    partial_value = jnp.dot(everyone, out_weight, preferred_element_type=jnp.float32).astype(jnp.bfloat16)
    mine = lax.all_to_all(partial_value, "cp", split_axis=0, concat_axis=1, tiled=True)
    return lax.psum_scatter(mine, "tp", scatter_dimension=1, tiled=True)


def solution(mesh):
    on_ring = mesh.shape["tp"] == 2 and mesh.shape["cp"] == 16
    return jax.shard_map(
        functools.partial(local, on_ring),
        mesh=mesh,
        in_specs=(P(None, "cp", "tp"), P(None, None, "tp"), P(None, "tp"), P("tp"), P("tp", "cp")),
        out_specs=P("cp", "tp"),
        check_vma=False,
    )
```

```python
import functools

import jax
import jax.numpy as jnp
from jax import lax
from jax.experimental import pallas as pl
from jax.experimental.pallas import tpu as pltpu
from jax.sharding import PartitionSpec as P

TAPS = 128
SHORT = 3
LANES = 128
SUB = 8


def from_behind(block, axis, distance):
    devices = range(lax.axis_size(axis))
    route = [(i - distance, i) for i in devices if i - distance in devices]
    return lax.ppermute(block, axis, route)


def conv_kernel(rows, width, feat_ref, halo_ref, edge_ref, short_ref, long_ref, skip_ref, out_ref, ext, prod):
    def strip(index, carry):
        lanes = pl.ds(pl.multiple_of(index * LANES, LANES), LANES)
        shorted = []
        for i in range(3):
            ext[i, pl.ds(0, SUB), :] = edge_ref[i, :, lanes].astype(jnp.float32)
            ext[i, pl.ds(SUB, rows), :] = feat_ref[i, :, lanes].astype(jnp.float32)
            total = short_ref[i, pl.ds(0, 1), lanes] * ext[i, pl.ds(SUB, rows), :]
            for lag in range(1, SHORT):
                total = total + short_ref[i, pl.ds(lag, 1), lanes] * ext[i, pl.ds(SUB - lag, rows), :]
            shorted.append(total)
        product = shorted[1] * shorted[2]
        prod[pl.ds(0, TAPS), :] = halo_ref[:, lanes].astype(jnp.float32)
        prod[pl.ds(TAPS, rows), :] = product
        total = skip_ref[:, lanes] * product
        span = rows + TAPS - SUB
        for r in range(SUB):
            shifted = prod[pl.ds(SUB - r, span), :]
            for m in range(TAPS // SUB):
                begin = TAPS - SUB - SUB * m
                total = total + long_ref[pl.ds(SUB * m + r, 1), lanes] * shifted[begin:begin + rows]
        out_ref[pl.ds(0, rows), lanes] = (shorted[0] * total).astype(jnp.bfloat16)
        if out_ref.shape[0] > rows:
            out_ref[pl.ds(rows, out_ref.shape[0] - rows), lanes] = jnp.zeros(
                (out_ref.shape[0] - rows, LANES), jnp.bfloat16
            )
        return carry

    lax.fori_loop(0, width // LANES, strip, 0)


def gate_conv(features, halo, edge, short_filter, long_filter, skip_scale, out_rows):
    _, rows, channels = features.shape
    width = min(512, channels)
    return pl.pallas_call(
        functools.partial(conv_kernel, rows, width),
        grid=(channels // width,),
        out_shape=jax.ShapeDtypeStruct((out_rows, channels), jnp.bfloat16),
        in_specs=[
            pl.BlockSpec((3, rows, width), lambda c: (0, 0, c)),
            pl.BlockSpec((TAPS, width), lambda c: (0, c)),
            pl.BlockSpec((3, SUB, width), lambda c: (0, 0, c)),
            pl.BlockSpec((3, SHORT, width), lambda c: (0, 0, c)),
            pl.BlockSpec((TAPS, width), lambda c: (0, c)),
            pl.BlockSpec((1, width), lambda c: (0, c)),
        ],
        out_specs=pl.BlockSpec((out_rows, width), lambda c: (0, c)),
        scratch_shapes=[
            pltpu.VMEM((3, SUB + rows, LANES), jnp.float32),
            pltpu.VMEM((TAPS + rows, LANES), jnp.float32),
        ],
        compiler_params=pltpu.CompilerParams(vmem_limit_bytes=32 * 2**20),
        cost_estimate=pl.CostEstimate(
            flops=2 * TAPS * rows * channels, bytes_accessed=10 * rows * channels, transcendentals=0
        ),
        name="gate_conv",
    )(features, halo, edge, short_filter, long_filter, skip_scale.reshape(1, channels))


def halo_of(features, short_filter):
    rows = features.shape[1]
    tail = features[1:, rows - TAPS - SHORT + 1:, :].astype(jnp.float32)
    shorted = sum(
        short_filter[1:, lag, None, :] * tail[:, SHORT - 1 - lag:SHORT - 1 - lag + TAPS] for lag in range(SHORT)
    )
    product = (shorted[0] * shorted[1]).astype(jnp.bfloat16)
    return product, features[:, rows - SUB:, :]


def mixer_kernel(
    n, parts, feat_ref, short_ref, long_ref, skip_ref, weight_ref, out_ref,
    blocks, weights, kept, sent, other, summed, landed, totals, direct, edge_out, edge_in, tail_out, tail_in, ext, prod,
    own_sem, edge_sem, tail_send, tail_recv, block_send, block_recv, weight_send, weight_recv,
    tp_send, tp_recv, out_send, out_recv,
):
    t, cp = lax.axis_index("tp"), lax.axis_index("cp")
    rows = feat_ref.shape[1]
    padded, part = blocks.shape[2:]
    core, chip = cp % 2, cp // 2
    x, z = chip % 2, chip // 2
    depth = n // 2
    place = x * (n - 1 - z) + (1 - x) * z
    forth = 1 - 2 * core
    half_owner = chip // depth
    my_piece = (chip % depth) * 2 + t

    def cp_at(ring_place):
        r = (ring_place + 2 * n) % n
        rx = r // depth
        rz = rx * (n - 1 - r) + (1 - rx) * r
        return (rz * 2 + rx) * 2 + core

    def peer(a, b):
        return dict(device_id=(a, b), device_id_type=pl.DeviceIdType.MESH)

    ahead, behind = cp_at(place + forth), cp_at(place - forth)
    sibling = cp + 1 - 2 * core
    is_first, is_last = cp == 0, cp == 2 * n - 1

    barrier = pltpu.get_barrier_semaphore()
    for device in ((t, ahead), (t, behind), (t, sibling), (1 - t, cp)):
        pl.semaphore_signal(barrier, inc=1, **peer(*device))

    @pl.when(cp > 0)
    def _():
        pl.semaphore_signal(barrier, inc=1, **peer(t, cp - 1))

    def greet(i, carry):
        sender = (t * depth + i // 2) * 2 + core

        @pl.when(jnp.logical_or(i % 2 != t, sender != cp))
        def _():
            pl.semaphore_signal(barrier, inc=1, **peer(i % 2, sender))

        return carry

    lax.fori_loop(0, n, greet, 0)
    pl.semaphore_wait(barrier, 4 + n - 1 + (half_owner + t) % 2 + (2 * n - 1 - cp + 2 * n - 2) // (2 * n - 1))

    columns = pltpu.make_async_remote_copy(
        src_ref=weight_ref, dst_ref=weights.at[core], send_sem=weight_send, recv_sem=weight_recv, **peer(t, sibling)
    )
    own_columns = pltpu.make_async_copy(weight_ref, weights.at[core], own_sem)
    edge_copy = pltpu.make_async_remote_copy(
        src_ref=edge_out, dst_ref=edge_in, send_sem=edge_sem.at[0], recv_sem=edge_sem.at[1], **peer(t, cp + 1)
    )

    def tail_copy(p):
        return pltpu.make_async_remote_copy(
            src_ref=tail_out.at[p], dst_ref=tail_in.at[p], send_sem=tail_send.at[p], recv_sem=tail_recv.at[p],
            **peer(t, cp + 1),
        )

    def strip_of(index):
        return pl.ds(pl.multiple_of(index * LANES, LANES), LANES)

    strips = part // LANES

    def edges(index, carry):
        lanes = strip_of(index)
        q, k, v = (feat_ref[i, pl.ds(rows - SUB, SUB), lanes].astype(jnp.float32) for i in range(3))
        row = lax.broadcasted_iota(jnp.int32, (SUB, LANES), 0)
        kv = jnp.where(row >= SUB - 2, k, pltpu.roll(v, SUB - 2, 0))
        edge_out[:, lanes] = jnp.concatenate((q, kv), axis=0).astype(jnp.bfloat16)
        return carry

    lax.fori_loop(0, parts * strips, edges, 0)

    @pl.when(jnp.logical_not(is_last))
    def _():
        edge_copy.start()

    own_columns.start()

    def short(i, lanes, begin, count):
        total = short_ref[i, pl.ds(0, 1), lanes] * ext[i, pl.ds(SUB + begin, count), :]
        for lag in range(1, SHORT):
            total = total + short_ref[i, pl.ds(lag, 1), lanes] * ext[i, pl.ds(SUB + begin - lag, count), :]
        return total

    def tails(p, carry):
        def one(s, carry):
            lanes = strip_of(p * strips + s)
            for i in (1, 2):
                ext[i, pl.ds(SUB, rows), :] = feat_ref[i, :, lanes].astype(jnp.float32)
            product = short(1, lanes, rows - TAPS, TAPS) * short(2, lanes, rows - TAPS, TAPS)
            tail_out[p, :, strip_of(s)] = product.astype(jnp.bfloat16)
            return carry

        lax.fori_loop(0, strips, one, 0)

        @pl.when(jnp.logical_not(is_last))
        def _():
            tail_copy(p).start()

        return carry

    lax.fori_loop(0, parts, tails, 0)
    columns.start()

    @pl.when(is_first)
    def _():
        edge_in[...] = jnp.zeros_like(edge_in)
        tail_in[...] = jnp.zeros_like(tail_in)

    @pl.when(jnp.logical_not(is_first))
    def _():
        edge_copy.wait_recv()

    def extend(lanes, which):
        edge = edge_in[:, lanes].astype(jnp.float32)
        q, kv = edge[:SUB], edge[SUB:]
        ahead_rows = (q, kv, pltpu.roll(kv, 2, 0))
        for i in which:
            ext[i, pl.ds(0, SUB), :] = ahead_rows[i]
            ext[i, pl.ds(SUB, rows), :] = feat_ref[i, :, lanes].astype(jnp.float32)

    prod[pl.ds(0, SUB), :] = jnp.zeros((SUB, LANES), jnp.float32)

    def own_rows(index, carry):
        lanes = strip_of(index)
        extend(lanes, (1, 2))
        product = short(1, lanes, 0, rows) * short(2, lanes, 0, rows)
        prod[pl.ds(SUB, rows), :] = product
        total = skip_ref[:, lanes] * product
        for r in range(SUB):
            shifted = prod[pl.ds(SUB - r, rows), :]
            for m in range(TAPS // SUB):
                tap = long_ref[pl.ds(SUB * m + r, 1), lanes]
                rest = total[SUB * m:] + tap * shifted[:rows - SUB * m]
                total = jnp.concatenate((total[:SUB * m], rest), axis=0) if m else rest
        direct[:, lanes] = total
        return carry

    lax.fori_loop(0, parts * strips, own_rows, 0)

    def send_own(slot, p, device):
        return pltpu.make_async_remote_copy(
            src_ref=blocks.at[0, p], dst_ref=blocks.at[slot, p], send_sem=block_send.at[slot, p],
            recv_sem=block_recv.at[slot, p], **peer(t, device),
        )

    def pass_on(slot, p):
        odd = slot % 2
        return pltpu.make_async_remote_copy(
            src_ref=blocks.at[slot, p], dst_ref=blocks.at[slot + 2, p], send_sem=block_send.at[slot + 2, p],
            recv_sem=block_recv.at[slot + 2, p], **peer(t, odd * ahead + (1 - odd) * behind),
        )

    prod[pl.ds(TAPS, SUB), :] = jnp.zeros((SUB, LANES), jnp.float32)

    def gates(p, carry):
        @pl.when(jnp.logical_not(is_first))
        def _():
            tail_copy(p).wait_recv()

        def one(s, carry):
            lanes = strip_of(p * strips + s)
            prod[pl.ds(0, TAPS), :] = tail_in[p, :, strip_of(s)].astype(jnp.float32)
            total = direct[pl.ds(0, TAPS), lanes]
            for r in range(SUB):
                shifted = prod[pl.ds(SUB - r, TAPS), :]
                for m in range(TAPS // SUB):
                    tap = long_ref[pl.ds(SUB * m + r, 1), lanes]
                    count = SUB * (m + 1)
                    head = total[:count] + tap * shifted[TAPS - count:]
                    total = jnp.concatenate((head, total[count:]), axis=0) if count < TAPS else head
            extend(lanes, (0,))
            gate = short(0, lanes, 0, rows)
            later = jnp.concatenate(
                (gate[TAPS:] * direct[pl.ds(TAPS, rows - TAPS), lanes],
                 jnp.zeros((padded - rows, LANES), jnp.float32)), axis=0,
            )
            blocks[0, p, pl.ds(0, TAPS), strip_of(s)] = (gate[:TAPS] * total).astype(jnp.bfloat16)
            blocks[0, p, pl.ds(TAPS, padded - TAPS), strip_of(s)] = later.astype(jnp.bfloat16)
            return carry

        lax.fori_loop(0, strips, one, 0)
        send_own(1, p, ahead).start()
        send_own(2, p, behind).start()
        return carry

    lax.fori_loop(0, parts, gates, 0)

    own_columns.wait()
    columns.wait_recv()

    def tp_copy(slot):
        return pltpu.make_async_remote_copy(
            src_ref=sent.at[slot], dst_ref=other.at[slot], send_sem=tp_send.at[slot], recv_sem=tp_recv.at[slot],
            **peer(1 - t, cp),
        )

    def out_copy(slot):
        odd, step = slot % 2, (slot + 1) // 2
        return pltpu.make_async_remote_copy(
            src_ref=summed.at[slot], dst_ref=landed.at[my_piece], send_sem=out_send.at[slot],
            recv_sem=out_recv.at[my_piece], **peer(half_owner, cp_at(place + (1 - 2 * odd) * forth * step)),
        )

    width = weights.shape[2]
    tile = min(256, width)

    def multiply(slot, p, first):
        depth_rows = pl.ds(pl.multiple_of(p * part, part), part)

        def one(j, carry):
            lanes = pl.ds(pl.multiple_of(j * tile, tile), tile)
            for side in range(2):
                value = jnp.dot(
                    blocks[slot, p], weights[side, depth_rows, lanes], preferred_element_type=jnp.float32
                )
                if not first:
                    value = value + totals[slot % 2, side, :, lanes]
                totals[slot % 2, side, :, lanes] = value
            return carry

        lax.fori_loop(0, width // tile, one, 0)

    def emit(slot):
        sent[slot] = totals[slot % 2, 1 - t].astype(jnp.bfloat16)
        tp_copy(slot).start()
        kept[slot] = totals[slot % 2, t].astype(jnp.bfloat16)

    def finish(slot):
        tp_copy(slot).wait_recv()
        total = (kept[slot].astype(jnp.float32) + other[slot].astype(jnp.float32)).astype(jnp.bfloat16)
        stays = jnp.logical_and(slot == 0, half_owner == t)

        @pl.when(stays)
        def _():
            landed[my_piece] = total

        @pl.when(jnp.logical_not(stays))
        def _():
            summed[slot] = total
            out_copy(slot).start()

    def take(slot, p, first):
        pltpu.make_async_copy(blocks.at[slot, p], blocks.at[slot, p], block_recv.at[slot, p]).wait()

        @pl.when(slot + 2 < n)
        def _():
            pass_on(slot, p).start()

        multiply(slot, p, first)

    multiply(0, 0, True)
    lax.fori_loop(1, parts, lambda p, carry: (multiply(0, p, False), carry)[1], 0)
    emit(0)

    def pair(i, carry):
        odd, even = 2 * i - 1, 2 * i

        def both(p, first):
            take(odd, p, first)
            take(even, p, first)

        both(0, True)
        lax.fori_loop(1, parts, lambda p, carry: (both(p, False), carry)[1], 0)
        emit(odd)
        emit(even)
        finish(odd - 1)

        @pl.when(i > 1)
        def _():
            finish(odd - 2)

        return carry

    lax.fori_loop(1, depth, pair, 0)
    take(n - 1, 0, True)
    finish(n - 2)
    finish(n - 3)
    lax.fori_loop(1, parts, lambda p, carry: (take(n - 1, p, False), carry)[1], 0)
    emit(n - 1)
    finish(n - 1)

    columns.wait_send()

    @pl.when(jnp.logical_not(is_last))
    def _():
        edge_copy.wait_send()

    def drain_parts(p, carry):
        @pl.when(jnp.logical_not(is_last))
        def _():
            tail_copy(p).wait_send()

        send_own(1, p, ahead).wait_send()
        send_own(2, p, behind).wait_send()
        lax.fori_loop(1, n - 2, lambda slot, carry: (pass_on(slot, p).wait_send(), carry)[1], 0)
        return carry

    lax.fori_loop(0, parts, drain_parts, 0)

    def drain(slot, carry):
        tp_copy(slot).wait_send()

        @pl.when(jnp.logical_not(jnp.logical_and(slot == 0, half_owner == t)))
        def _():
            out_copy(slot).wait_send()

        return carry

    lax.fori_loop(0, n, drain, 0)
    for piece in range(n):
        @pl.when(jnp.logical_not(jnp.logical_and(piece == my_piece, half_owner == t)))
        def _():
            pltpu.make_async_copy(landed.at[piece], landed.at[piece], out_recv.at[piece]).wait()

        out_ref[:, pl.ds(piece * width, width)] = landed[piece, pl.ds(0, rows), :]


def mixer(features, short_filter, long_filter, skip_scale, out_weight, n):
    _, rows, channels = features.shape
    padded = -(-rows // 16) * 16
    width = out_weight.shape[1]
    parts = 4
    part = channels // parts
    kind = jnp.bfloat16
    dma = pltpu.SemaphoreType.DMA
    whole = pl.BlockSpec(memory_space=pltpu.VMEM)
    return pl.pallas_call(
        functools.partial(mixer_kernel, n, parts),
        out_shape=jax.ShapeDtypeStruct((rows, n * width), kind),
        in_specs=[whole] * 4 + [pl.BlockSpec(memory_space=pl.ANY)],
        out_specs=whole,
        scratch_shapes=[
            pltpu.VMEM((n, parts, padded, part), kind),
            pltpu.VMEM((2, channels, width), kind),
            *[pltpu.VMEM((n, padded, width), kind)] * 5,
            pltpu.VMEM((2, 2, padded, width), jnp.float32),
            pltpu.VMEM((rows, channels), jnp.float32),
            *[pltpu.VMEM((2 * SUB, channels), kind)] * 2,
            *[pltpu.VMEM((parts, TAPS, part), kind)] * 2,
            pltpu.VMEM((3, SUB + rows, LANES), jnp.float32),
            pltpu.VMEM((TAPS + 2 * SUB, LANES), jnp.float32),
            dma, dma((2,)), dma((parts,)), dma((parts,)), dma((n, parts)), dma((n, parts)), dma, dma,
            dma((n,)), dma((n,)), dma((n,)), dma((n,)),
        ],
        compiler_params=pltpu.CompilerParams(
            collective_id=0, has_side_effects=True, vmem_limit_bytes=56 * 2**20
        ),
        cost_estimate=pl.CostEstimate(
            flops=4 * n * padded * channels * width, bytes_accessed=4 * channels * width, transcendentals=0
        ),
        name="mixer",
    )(features, short_filter, long_filter, skip_scale.reshape(1, channels), out_weight)


def local(on_ring, features, short_filter, long_filter, skip_scale, out_weight):
    rows = features.shape[1]
    if on_ring:
        return mixer(features, short_filter, long_filter, skip_scale, out_weight, lax.axis_size("cp") // 2)
    product, edge = halo_of(features, short_filter)
    halo = from_behind(product, "cp", 1)
    edge = from_behind(edge, "cp", 1)
    gated = gate_conv(features, halo, edge, short_filter, long_filter, skip_scale, rows)
    everyone = lax.all_gather(gated, "cp", axis=0, tiled=True)
    partial_value = jnp.dot(everyone, out_weight, preferred_element_type=jnp.float32).astype(jnp.bfloat16)
    mine = lax.all_to_all(partial_value, "cp", split_axis=0, concat_axis=1, tiled=True)
    return lax.psum_scatter(mine, "tp", scatter_dimension=1, tiled=True)


def solution(mesh):
    on_ring = mesh.shape["tp"] == 2 and mesh.shape["cp"] == 16
    return jax.shard_map(
        functools.partial(local, on_ring),
        mesh=mesh,
        in_specs=(P(None, "cp", "tp"), P(None, None, "tp"), P(None, "tp"), P("tp"), P("tp", "cp")),
        out_specs=P("cp", "tp"),
        check_vma=False,
    )
```

```python
import functools

import jax
import jax.numpy as jnp
from jax import lax
from jax.experimental import pallas as pl
from jax.experimental.pallas import tpu as pltpu
from jax.sharding import PartitionSpec as P

TAPS = 128
SHORT = 3
LANES = 128
SUB = 8


def from_behind(block, axis, distance):
    devices = range(lax.axis_size(axis))
    route = [(i - distance, i) for i in devices if i - distance in devices]
    return lax.ppermute(block, axis, route)


def conv_kernel(rows, width, feat_ref, halo_ref, edge_ref, short_ref, long_ref, skip_ref, out_ref, ext, prod):
    def strip(index, carry):
        lanes = pl.ds(pl.multiple_of(index * LANES, LANES), LANES)
        shorted = []
        for i in range(3):
            ext[i, pl.ds(0, SUB), :] = edge_ref[i, :, lanes].astype(jnp.float32)
            ext[i, pl.ds(SUB, rows), :] = feat_ref[i, :, lanes].astype(jnp.float32)
            total = short_ref[i, pl.ds(0, 1), lanes] * ext[i, pl.ds(SUB, rows), :]
            for lag in range(1, SHORT):
                total = total + short_ref[i, pl.ds(lag, 1), lanes] * ext[i, pl.ds(SUB - lag, rows), :]
            shorted.append(total)
        product = shorted[1] * shorted[2]
        prod[pl.ds(0, TAPS), :] = halo_ref[:, lanes].astype(jnp.float32)
        prod[pl.ds(TAPS, rows), :] = product
        total = skip_ref[:, lanes] * product
        span = rows + TAPS - SUB
        for r in range(SUB):
            shifted = prod[pl.ds(SUB - r, span), :]
            for m in range(TAPS // SUB):
                begin = TAPS - SUB - SUB * m
                total = total + long_ref[pl.ds(SUB * m + r, 1), lanes] * shifted[begin:begin + rows]
        out_ref[pl.ds(0, rows), lanes] = (shorted[0] * total).astype(jnp.bfloat16)
        if out_ref.shape[0] > rows:
            out_ref[pl.ds(rows, out_ref.shape[0] - rows), lanes] = jnp.zeros(
                (out_ref.shape[0] - rows, LANES), jnp.bfloat16
            )
        return carry

    lax.fori_loop(0, width // LANES, strip, 0)


def gate_conv(features, halo, edge, short_filter, long_filter, skip_scale, out_rows):
    _, rows, channels = features.shape
    width = min(512, channels)
    return pl.pallas_call(
        functools.partial(conv_kernel, rows, width),
        grid=(channels // width,),
        out_shape=jax.ShapeDtypeStruct((out_rows, channels), jnp.bfloat16),
        in_specs=[
            pl.BlockSpec((3, rows, width), lambda c: (0, 0, c)),
            pl.BlockSpec((TAPS, width), lambda c: (0, c)),
            pl.BlockSpec((3, SUB, width), lambda c: (0, 0, c)),
            pl.BlockSpec((3, SHORT, width), lambda c: (0, 0, c)),
            pl.BlockSpec((TAPS, width), lambda c: (0, c)),
            pl.BlockSpec((1, width), lambda c: (0, c)),
        ],
        out_specs=pl.BlockSpec((out_rows, width), lambda c: (0, c)),
        scratch_shapes=[
            pltpu.VMEM((3, SUB + rows, LANES), jnp.float32),
            pltpu.VMEM((TAPS + rows, LANES), jnp.float32),
        ],
        compiler_params=pltpu.CompilerParams(vmem_limit_bytes=32 * 2**20),
        cost_estimate=pl.CostEstimate(
            flops=2 * TAPS * rows * channels, bytes_accessed=10 * rows * channels, transcendentals=0
        ),
        name="gate_conv",
    )(features, halo, edge, short_filter, long_filter, skip_scale.reshape(1, channels))


def halo_of(features, short_filter):
    rows = features.shape[1]
    tail = features[1:, rows - TAPS - SHORT + 1:, :].astype(jnp.float32)
    shorted = sum(
        short_filter[1:, lag, None, :] * tail[:, SHORT - 1 - lag:SHORT - 1 - lag + TAPS] for lag in range(SHORT)
    )
    product = (shorted[0] * shorted[1]).astype(jnp.bfloat16)
    return product, features[:, rows - SUB:, :]


def mixer_kernel(
    n, parts, feat_ref, short_ref, long_ref, skip_ref, weight_ref, out_ref,
    blocks, weights, kept, sent, other, summed, landed, relayed, totals, direct, edge_out, edge_in, tail_out, tail_in,
    ext, prod, before,
    own_sem, edge_sem, tail_send, tail_recv, block_send, block_recv, weight_send, weight_recv,
    tp_send, tp_recv, out_send, out_recv, relay_send, relay_recv,
):
    t, cp = lax.axis_index("tp"), lax.axis_index("cp")
    rows = feat_ref.shape[1]
    padded, part = blocks.shape[2:]
    core, chip = cp % 2, cp // 2
    x, z = chip % 2, chip // 2
    depth = n // 2
    place = x * (n - 1 - z) + (1 - x) * z
    forth = 1 - 2 * core

    def cp_at(ring_place):
        r = (ring_place + 2 * n) % n
        rx = r // depth
        rz = rx * (n - 1 - r) + (1 - rx) * r
        return (rz * 2 + rx) * 2 + core

    def peer(a, b):
        return dict(device_id=(a, b), device_id_type=pl.DeviceIdType.MESH)

    ahead, behind = cp_at(place + forth), cp_at(place - forth)
    sibling = cp + 1 - 2 * core
    is_first, is_last = cp == 0, cp == 2 * n - 1

    barrier = pltpu.get_barrier_semaphore()
    for device in ((t, sibling), (1 - t, cp)):
        pl.semaphore_signal(barrier, inc=1, **peer(*device))

    @pl.when(cp > 0)
    def _():
        pl.semaphore_signal(barrier, inc=1, **peer(t, cp - 1))

    def greet(i, carry):
        pl.semaphore_signal(barrier, inc=1, **peer(t, cp_at(place + i)))
        return carry

    lax.fori_loop(1, n, greet, 0)
    pl.semaphore_wait(barrier, 2 + n - 1 + (2 * n - 1 - cp + 2 * n - 2) // (2 * n - 1))

    columns = pltpu.make_async_remote_copy(
        src_ref=weight_ref, dst_ref=weights.at[core], send_sem=weight_send, recv_sem=weight_recv, **peer(t, sibling)
    )
    own_columns = pltpu.make_async_copy(weight_ref, weights.at[core], own_sem)
    edge_copy = pltpu.make_async_remote_copy(
        src_ref=edge_out, dst_ref=edge_in, send_sem=edge_sem.at[0], recv_sem=edge_sem.at[1], **peer(t, cp + 1)
    )

    def tail_copy(p):
        return pltpu.make_async_remote_copy(
            src_ref=tail_out.at[p], dst_ref=tail_in.at[p], send_sem=tail_send.at[p], recv_sem=tail_recv.at[p],
            **peer(t, cp + 1),
        )

    def strip_of(index):
        return pl.ds(pl.multiple_of(index * LANES, LANES), LANES)

    strips = part // LANES

    def edges(index, carry):
        lanes = strip_of(index)
        q, k, v = (feat_ref[i, pl.ds(rows - SUB, SUB), lanes].astype(jnp.float32) for i in range(3))
        row = lax.broadcasted_iota(jnp.int32, (SUB, LANES), 0)
        kv = jnp.where(row >= SUB - 2, k, pltpu.roll(v, SUB - 2, 0))
        edge_out[:, lanes] = jnp.concatenate((q, kv), axis=0).astype(jnp.bfloat16)
        return carry

    lax.fori_loop(0, parts * strips, edges, 0)

    @pl.when(jnp.logical_not(is_last))
    def _():
        edge_copy.start()

    own_columns.start()

    def short(i, lanes, begin, count):
        total = short_ref[i, pl.ds(0, 1), lanes] * ext[i, pl.ds(SUB + begin, count), :]
        for lag in range(1, SHORT):
            total = total + short_ref[i, pl.ds(lag, 1), lanes] * ext[i, pl.ds(SUB + begin - lag, count), :]
        return total

    def tails(p, carry):
        def one(s, carry):
            lanes = strip_of(p * strips + s)
            for i in (1, 2):
                ext[i, pl.ds(SUB, rows), :] = feat_ref[i, :, lanes].astype(jnp.float32)
            product = short(1, lanes, rows - TAPS, TAPS) * short(2, lanes, rows - TAPS, TAPS)
            tail_out[p, :, strip_of(s)] = product.astype(jnp.bfloat16)
            return carry

        lax.fori_loop(0, strips, one, 0)

        @pl.when(jnp.logical_not(is_last))
        def _():
            tail_copy(p).start()

        return carry

    lax.fori_loop(0, parts, tails, 0)
    columns.start()

    @pl.when(is_first)
    def _():
        edge_in[...] = jnp.zeros_like(edge_in)
        tail_in[...] = jnp.zeros_like(tail_in)

    @pl.when(jnp.logical_not(is_first))
    def _():
        edge_copy.wait_recv()

    def extend(lanes, which):
        edge = edge_in[:, lanes].astype(jnp.float32)
        q, kv = edge[:SUB], edge[SUB:]
        ahead_rows = (q, kv, pltpu.roll(kv, 2, 0))
        for i in which:
            ext[i, pl.ds(0, SUB), :] = ahead_rows[i]
            ext[i, pl.ds(SUB, rows), :] = feat_ref[i, :, lanes].astype(jnp.float32)

    prod[pl.ds(0, SUB), :] = jnp.zeros((SUB, LANES), jnp.float32)

    def own_strip(index, carry):
        lanes = strip_of(index)
        extend(lanes, (1, 2))
        product = short(1, lanes, 0, rows) * short(2, lanes, 0, rows)
        prod[pl.ds(SUB, rows), :] = product
        total = skip_ref[:, lanes] * product
        for r in range(SUB):
            shifted = prod[pl.ds(SUB - r, rows), :]
            for m in range(TAPS // SUB):
                tap = long_ref[pl.ds(SUB * m + r, 1), lanes]
                rest = total[SUB * m:] + tap * shifted[:rows - SUB * m]
                total = jnp.concatenate((total[:SUB * m], rest), axis=0) if m else rest
        direct[:, lanes] = total
        return carry

    def own_rows(p):
        lax.fori_loop(p * strips, (p + 1) * strips, own_strip, 0)

    def send_own(slot, p, device):
        return pltpu.make_async_remote_copy(
            src_ref=blocks.at[0, p], dst_ref=blocks.at[slot, p], send_sem=block_send.at[slot, p],
            recv_sem=block_recv.at[slot, p], **peer(t, device),
        )

    def pass_on(slot, p):
        odd = slot % 2
        return pltpu.make_async_remote_copy(
            src_ref=blocks.at[slot, p], dst_ref=blocks.at[slot + 2, p], send_sem=block_send.at[slot + 2, p],
            recv_sem=block_recv.at[slot + 2, p], **peer(t, odd * ahead + (1 - odd) * behind),
        )

    before[pl.ds(TAPS, SUB), :] = jnp.zeros((SUB, LANES), jnp.float32)

    def gates(p, carry):
        @pl.when(p + 1 < parts)
        def _():
            own_rows(p + 1)

        @pl.when(jnp.logical_not(is_first))
        def _():
            tail_copy(p).wait_recv()

        def one(s, carry):
            lanes = strip_of(p * strips + s)
            before[pl.ds(0, TAPS), :] = tail_in[p, :, strip_of(s)].astype(jnp.float32)
            total = direct[pl.ds(0, TAPS), lanes]
            for r in range(SUB):
                shifted = before[pl.ds(SUB - r, TAPS), :]
                for m in range(TAPS // SUB):
                    tap = long_ref[pl.ds(SUB * m + r, 1), lanes]
                    count = SUB * (m + 1)
                    head = total[:count] + tap * shifted[TAPS - count:]
                    total = jnp.concatenate((head, total[count:]), axis=0) if count < TAPS else head
            extend(lanes, (0,))
            gate = short(0, lanes, 0, rows)
            later = jnp.concatenate(
                (gate[TAPS:] * direct[pl.ds(TAPS, rows - TAPS), lanes],
                 jnp.zeros((padded - rows, LANES), jnp.float32)), axis=0,
            )
            blocks[0, p, pl.ds(0, TAPS), strip_of(s)] = (gate[:TAPS] * total).astype(jnp.bfloat16)
            blocks[0, p, pl.ds(TAPS, padded - TAPS), strip_of(s)] = later.astype(jnp.bfloat16)
            return carry

        lax.fori_loop(0, strips, one, 0)
        send_own(1, p, ahead).start()
        send_own(2, p, behind).start()
        return carry

    own_rows(0)
    lax.fori_loop(0, parts, gates, 0)

    own_columns.wait()
    columns.wait_recv()

    def tp_copy(slot):
        return pltpu.make_async_remote_copy(
            src_ref=sent.at[slot], dst_ref=other.at[slot], send_sem=tp_send.at[slot], recv_sem=tp_recv.at[slot],
            **peer(1 - t, cp),
        )

    def out_copy(slot):
        odd, step = slot % 2, (slot + 1) // 2
        return pltpu.make_async_remote_copy(
            src_ref=summed.at[slot], dst_ref=landed.at[chip], send_sem=out_send.at[slot],
            recv_sem=out_recv.at[chip], **peer(t, cp_at(place + (1 - 2 * odd) * forth * step)),
        )

    def arrived(sender):
        pltpu.make_async_copy(landed.at[sender], landed.at[sender], out_recv.at[sender]).wait()

    def relay_copy(sender):
        return pltpu.make_async_remote_copy(
            src_ref=landed.at[sender], dst_ref=relayed.at[sender % depth], send_sem=relay_send.at[sender % depth],
            recv_sem=relay_recv.at[sender % depth], **peer(1 - t, cp),
        )

    def relay(distance):
        for way in ((1,) if distance in (0, depth) else (1, -1)):
            sender = cp_at(place + way * distance) // 2

            @pl.when(sender // depth != t)
            def _():
                if distance:
                    arrived(sender)
                relay_copy(sender).start()

    width = weights.shape[2]
    tile = min(256, width)

    def multiply(slot, p, first):
        depth_rows = pl.ds(pl.multiple_of(p * part, part), part)

        def one(j, carry):
            lanes = pl.ds(pl.multiple_of(j * tile, tile), tile)
            for side in range(2):
                value = jnp.dot(
                    blocks[slot, p], weights[side, depth_rows, lanes], preferred_element_type=jnp.float32
                )
                if not first:
                    value = value + totals[slot % 2, side, :, lanes]
                totals[slot % 2, side, :, lanes] = value
            return carry

        lax.fori_loop(0, width // tile, one, 0)

    def emit(slot):
        sent[slot] = totals[slot % 2, 1 - t].astype(jnp.bfloat16)
        tp_copy(slot).start()
        kept[slot] = totals[slot % 2, t].astype(jnp.bfloat16)

    def finish(slot):
        tp_copy(slot).wait_recv()
        total = (kept[slot].astype(jnp.float32) + other[slot].astype(jnp.float32)).astype(jnp.bfloat16)
        if isinstance(slot, int) and slot == 0:
            landed[chip] = total
        else:
            summed[slot] = total
            out_copy(slot).start()

    def take(slot, p, first):
        pltpu.make_async_copy(blocks.at[slot, p], blocks.at[slot, p], block_recv.at[slot, p]).wait()

        @pl.when(slot + 2 < n)
        def _():
            pass_on(slot, p).start()

        multiply(slot, p, first)

    multiply(0, 0, True)
    lax.fori_loop(1, parts, lambda p, carry: (multiply(0, p, False), carry)[1], 0)
    emit(0)

    def pair(i):
        odd, even = 2 * i - 1, 2 * i

        def both(p, first):
            take(odd, p, first)
            take(even, p, first)

        both(0, True)
        lax.fori_loop(1, parts, lambda p, carry: (both(p, False), carry)[1], 0)
        emit(odd)
        emit(even)

    pair(1)
    finish(0)
    relay(0)
    for i in range(2, depth):
        pair(i)
        finish(2 * i - 2)
        finish(2 * i - 3)
        if i > 2:
            relay(i - 2)
    take(n - 1, 0, True)
    finish(n - 2)
    finish(n - 3)
    relay(depth - 2)
    lax.fori_loop(1, parts, lambda p, carry: (take(n - 1, p, False), carry)[1], 0)
    emit(n - 1)
    finish(n - 1)
    relay(depth - 1)
    relay(depth)

    columns.wait_send()

    @pl.when(jnp.logical_not(is_last))
    def _():
        edge_copy.wait_send()

    def drain_parts(p, carry):
        @pl.when(jnp.logical_not(is_last))
        def _():
            tail_copy(p).wait_send()

        send_own(1, p, ahead).wait_send()
        send_own(2, p, behind).wait_send()
        lax.fori_loop(1, n - 2, lambda slot, carry: (pass_on(slot, p).wait_send(), carry)[1], 0)
        return carry

    lax.fori_loop(0, parts, drain_parts, 0)

    def drain(slot, carry):
        tp_copy(slot).wait_send()

        @pl.when(slot > 0)
        def _():
            out_copy(slot).wait_send()

        return carry

    lax.fori_loop(0, n, drain, 0)

    def columns_of(piece):
        return pl.ds(pl.multiple_of(piece * width, width), width)

    for m in range(depth):
        sender = t * depth + m

        @pl.when(sender != chip)
        def _():
            arrived(sender)

        out_ref[:, columns_of(2 * m + t)] = landed[sender, pl.ds(0, rows), :]
    for m in range(depth):
        relay_copy((1 - t) * depth + m).wait()
        out_ref[:, columns_of(2 * m + 1 - t)] = relayed[m, pl.ds(0, rows), :]


def mixer(features, short_filter, long_filter, skip_scale, out_weight, n):
    _, rows, channels = features.shape
    padded = -(-rows // 16) * 16
    width = out_weight.shape[1]
    parts = 4
    part = channels // parts
    kind = jnp.bfloat16
    dma = pltpu.SemaphoreType.DMA
    whole = pl.BlockSpec(memory_space=pltpu.VMEM)
    return pl.pallas_call(
        functools.partial(mixer_kernel, n, parts),
        out_shape=jax.ShapeDtypeStruct((rows, n * width), kind),
        in_specs=[whole] * 4 + [pl.BlockSpec(memory_space=pl.ANY)],
        out_specs=whole,
        scratch_shapes=[
            pltpu.VMEM((n, parts, padded, part), kind),
            pltpu.VMEM((2, channels, width), kind),
            *[pltpu.VMEM((n, padded, width), kind)] * 5,
            pltpu.VMEM((n // 2, padded, width), kind),
            pltpu.VMEM((2, 2, padded, width), jnp.float32),
            pltpu.VMEM((rows, channels), jnp.float32),
            *[pltpu.VMEM((2 * SUB, channels), kind)] * 2,
            *[pltpu.VMEM((parts, TAPS, part), kind)] * 2,
            pltpu.VMEM((3, SUB + rows, LANES), jnp.float32),
            pltpu.VMEM((SUB + rows, LANES), jnp.float32),
            pltpu.VMEM((TAPS + SUB, LANES), jnp.float32),
            dma, dma((2,)), dma((parts,)), dma((parts,)), dma((n, parts)), dma((n, parts)), dma, dma,
            dma((n,)), dma((n,)), dma((n,)), dma((n,)), dma((n // 2,)), dma((n // 2,)),
        ],
        compiler_params=pltpu.CompilerParams(
            collective_id=0, has_side_effects=True, vmem_limit_bytes=56 * 2**20
        ),
        cost_estimate=pl.CostEstimate(
            flops=4 * n * padded * channels * width, bytes_accessed=4 * channels * width, transcendentals=0
        ),
        name="mixer",
    )(features, short_filter, long_filter, skip_scale.reshape(1, channels), out_weight)


def local(on_ring, features, short_filter, long_filter, skip_scale, out_weight):
    rows = features.shape[1]
    if on_ring:
        return mixer(features, short_filter, long_filter, skip_scale, out_weight, lax.axis_size("cp") // 2)
    product, edge = halo_of(features, short_filter)
    halo = from_behind(product, "cp", 1)
    edge = from_behind(edge, "cp", 1)
    gated = gate_conv(features, halo, edge, short_filter, long_filter, skip_scale, rows)
    everyone = lax.all_gather(gated, "cp", axis=0, tiled=True)
    partial_value = jnp.dot(everyone, out_weight, preferred_element_type=jnp.float32).astype(jnp.bfloat16)
    mine = lax.all_to_all(partial_value, "cp", split_axis=0, concat_axis=1, tiled=True)
    return lax.psum_scatter(mine, "tp", scatter_dimension=1, tiled=True)


def solution(mesh):
    on_ring = mesh.shape["tp"] == 2 and mesh.shape["cp"] == 16
    return jax.shard_map(
        functools.partial(local, on_ring),
        mesh=mesh,
        in_specs=(P(None, "cp", "tp"), P(None, None, "tp"), P(None, "tp"), P("tp"), P("tp", "cp")),
        out_specs=P("cp", "tp"),
        check_vma=False,
    )
```

```python
import functools

import jax
import jax.numpy as jnp
from jax import lax
from jax.experimental import pallas as pl
from jax.experimental.pallas import tpu as pltpu
from jax.sharding import PartitionSpec as P

TAPS = 128
SHORT = 3
LANES = 128
SUB = 8


def from_behind(block, axis, distance):
    devices = range(lax.axis_size(axis))
    route = [(i - distance, i) for i in devices if i - distance in devices]
    return lax.ppermute(block, axis, route)


def conv_kernel(rows, width, feat_ref, halo_ref, edge_ref, short_ref, long_ref, skip_ref, out_ref, ext, prod):
    def strip(index, carry):
        lanes = pl.ds(pl.multiple_of(index * LANES, LANES), LANES)
        shorted = []
        for i in range(3):
            ext[i, pl.ds(0, SUB), :] = edge_ref[i, :, lanes].astype(jnp.float32)
            ext[i, pl.ds(SUB, rows), :] = feat_ref[i, :, lanes].astype(jnp.float32)
            total = short_ref[i, pl.ds(0, 1), lanes] * ext[i, pl.ds(SUB, rows), :]
            for lag in range(1, SHORT):
                total = total + short_ref[i, pl.ds(lag, 1), lanes] * ext[i, pl.ds(SUB - lag, rows), :]
            shorted.append(total)
        product = shorted[1] * shorted[2]
        prod[pl.ds(0, TAPS), :] = halo_ref[:, lanes].astype(jnp.float32)
        prod[pl.ds(TAPS, rows), :] = product
        total = skip_ref[:, lanes] * product
        span = rows + TAPS - SUB
        for r in range(SUB):
            shifted = prod[pl.ds(SUB - r, span), :]
            for m in range(TAPS // SUB):
                begin = TAPS - SUB - SUB * m
                total = total + long_ref[pl.ds(SUB * m + r, 1), lanes] * shifted[begin:begin + rows]
        out_ref[pl.ds(0, rows), lanes] = (shorted[0] * total).astype(jnp.bfloat16)
        if out_ref.shape[0] > rows:
            out_ref[pl.ds(rows, out_ref.shape[0] - rows), lanes] = jnp.zeros(
                (out_ref.shape[0] - rows, LANES), jnp.bfloat16
            )
        return carry

    lax.fori_loop(0, width // LANES, strip, 0)


def gate_conv(features, halo, edge, short_filter, long_filter, skip_scale, out_rows):
    _, rows, channels = features.shape
    width = min(512, channels)
    return pl.pallas_call(
        functools.partial(conv_kernel, rows, width),
        grid=(channels // width,),
        out_shape=jax.ShapeDtypeStruct((out_rows, channels), jnp.bfloat16),
        in_specs=[
            pl.BlockSpec((3, rows, width), lambda c: (0, 0, c)),
            pl.BlockSpec((TAPS, width), lambda c: (0, c)),
            pl.BlockSpec((3, SUB, width), lambda c: (0, 0, c)),
            pl.BlockSpec((3, SHORT, width), lambda c: (0, 0, c)),
            pl.BlockSpec((TAPS, width), lambda c: (0, c)),
            pl.BlockSpec((1, width), lambda c: (0, c)),
        ],
        out_specs=pl.BlockSpec((out_rows, width), lambda c: (0, c)),
        scratch_shapes=[
            pltpu.VMEM((3, SUB + rows, LANES), jnp.float32),
            pltpu.VMEM((TAPS + rows, LANES), jnp.float32),
        ],
        compiler_params=pltpu.CompilerParams(vmem_limit_bytes=32 * 2**20),
        cost_estimate=pl.CostEstimate(
            flops=2 * TAPS * rows * channels, bytes_accessed=10 * rows * channels, transcendentals=0
        ),
        name="gate_conv",
    )(features, halo, edge, short_filter, long_filter, skip_scale.reshape(1, channels))


def halo_of(features, short_filter):
    rows = features.shape[1]
    tail = features[1:, rows - TAPS - SHORT + 1:, :].astype(jnp.float32)
    shorted = sum(
        short_filter[1:, lag, None, :] * tail[:, SHORT - 1 - lag:SHORT - 1 - lag + TAPS] for lag in range(SHORT)
    )
    product = (shorted[0] * shorted[1]).astype(jnp.bfloat16)
    return product, features[:, rows - SUB:, :]


def mixer_kernel(
    n, parts, feat_ref, short_ref, long_ref, skip_ref, weight_ref, out_ref,
    blocks, weights, kept, sent, other, summed, landed, totals, direct, edge_out, edge_in, tail_out, tail_in, ext, prod, before,
    own_sem, edge_sem, tail_send, tail_recv, block_send, block_recv, weight_send, weight_recv,
    tp_send, tp_recv, out_send, out_recv,
):
    t, cp = lax.axis_index("tp"), lax.axis_index("cp")
    rows = feat_ref.shape[1]
    part = blocks.shape[3]
    core, chip = cp % 2, cp // 2
    x, z = chip % 2, chip // 2
    depth = n // 2
    place = x * (n - 1 - z) + (1 - x) * z
    forth = 1 - 2 * core
    half_owner = chip // depth
    my_piece = (chip % depth) * 2 + t

    def cp_at(ring_place):
        r = (ring_place + 2 * n) % n
        rx = r // depth
        rz = rx * (n - 1 - r) + (1 - rx) * r
        return (rz * 2 + rx) * 2 + core

    def peer(a, b):
        return dict(device_id=(a, b), device_id_type=pl.DeviceIdType.MESH)

    ahead, behind = cp_at(place + forth), cp_at(place - forth)
    sibling = cp + 1 - 2 * core
    across = cp_at(n - 1 - place)
    takes_seventh, takes_sixth = place % depth == 2 - core, place % depth == 1 + core
    is_first, is_last = cp == 0, cp == 2 * n - 1

    barrier = pltpu.get_barrier_semaphore()
    for device in ((t, ahead), (t, behind), (t, sibling), (1 - t, cp)):
        pl.semaphore_signal(barrier, inc=1, **peer(*device))

    @pl.when(jnp.logical_or(takes_seventh, takes_sixth))
    def _():
        pl.semaphore_signal(barrier, inc=1, **peer(t, across))

    @pl.when(cp > 0)
    def _():
        pl.semaphore_signal(barrier, inc=1, **peer(t, cp - 1))

    def greet(i, carry):
        sender = (t * depth + i // 2) * 2 + core

        @pl.when(jnp.logical_or(i % 2 != t, sender != cp))
        def _():
            pl.semaphore_signal(barrier, inc=1, **peer(i % 2, sender))

        return carry

    lax.fori_loop(0, n, greet, 0)
    has_chord, has_next = (place % depth + 1) // 2 % 2, (4 * n - 3 - cp) // (2 * n - 1)
    pl.semaphore_wait(barrier, 4 + n - 1 + (half_owner + t) % 2 + has_chord + has_next)

    columns = pltpu.make_async_remote_copy(
        src_ref=weight_ref, dst_ref=weights.at[core], send_sem=weight_send, recv_sem=weight_recv, **peer(t, sibling)
    )
    own_columns = pltpu.make_async_copy(weight_ref, weights.at[core], own_sem)
    edge_copy = pltpu.make_async_remote_copy(
        src_ref=edge_out, dst_ref=edge_in, send_sem=edge_sem.at[0], recv_sem=edge_sem.at[1], **peer(t, cp + 1)
    )

    def tail_copy(p):
        return pltpu.make_async_remote_copy(
            src_ref=tail_out.at[p], dst_ref=tail_in.at[p], send_sem=tail_send.at[p], recv_sem=tail_recv.at[p],
            **peer(t, cp + 1),
        )

    def strip_of(index):
        return pl.ds(pl.multiple_of(index * LANES, LANES), LANES)

    strips = part // LANES

    def edges(index, carry):
        lanes = strip_of(index)
        q, k, v = (feat_ref[i, pl.ds(rows - SUB, SUB), lanes].astype(jnp.float32) for i in range(3))
        row = lax.broadcasted_iota(jnp.int32, (SUB, LANES), 0)
        kv = jnp.where(row >= SUB - 2, k, pltpu.roll(v, SUB - 2, 0))
        edge_out[:, lanes] = jnp.concatenate((q, kv), axis=0).astype(jnp.bfloat16)
        return carry

    lax.fori_loop(0, parts * strips, edges, 0)

    @pl.when(jnp.logical_not(is_last))
    def _():
        edge_copy.start()

    own_columns.start()

    def short(i, lanes, begin, count):
        total = short_ref[i, pl.ds(0, 1), lanes] * ext[i, pl.ds(SUB + begin, count), :]
        for lag in range(1, SHORT):
            total = total + short_ref[i, pl.ds(lag, 1), lanes] * ext[i, pl.ds(SUB + begin - lag, count), :]
        return total

    def tails(p, carry):
        def one(s, carry):
            lanes = strip_of(p * strips + s)
            for i in (1, 2):
                ext[i, pl.ds(SUB, rows), :] = feat_ref[i, :, lanes].astype(jnp.float32)
            product = short(1, lanes, rows - TAPS, TAPS) * short(2, lanes, rows - TAPS, TAPS)
            tail_out[p, :, strip_of(s)] = product.astype(jnp.bfloat16)
            return carry

        lax.fori_loop(0, strips, one, 0)

        @pl.when(jnp.logical_not(is_last))
        def _():
            tail_copy(p).start()

        return carry

    lax.fori_loop(0, parts, tails, 0)
    columns.start()

    @pl.when(is_first)
    def _():
        edge_in[...] = jnp.zeros_like(edge_in)
        tail_in[...] = jnp.zeros_like(tail_in)

    @pl.when(jnp.logical_not(is_first))
    def _():
        edge_copy.wait_recv()

    def extend(lanes, which):
        edge = edge_in[:, lanes].astype(jnp.float32)
        q, kv = edge[:SUB], edge[SUB:]
        ahead_rows = (q, kv, pltpu.roll(kv, 2, 0))
        for i in which:
            ext[i, pl.ds(0, SUB), :] = ahead_rows[i]
            ext[i, pl.ds(SUB, rows), :] = feat_ref[i, :, lanes].astype(jnp.float32)

    prod[pl.ds(0, SUB), :] = jnp.zeros((SUB, LANES), jnp.float32)

    def own_strip(index, carry):
        lanes = strip_of(index)
        extend(lanes, (1, 2))
        product = short(1, lanes, 0, rows) * short(2, lanes, 0, rows)
        prod[pl.ds(SUB, rows), :] = product
        total = skip_ref[:, lanes] * product
        for r in range(SUB):
            shifted = prod[pl.ds(SUB - r, rows), :]
            for m in range(TAPS // SUB):
                tap = long_ref[pl.ds(SUB * m + r, 1), lanes]
                rest = total[SUB * m:] + tap * shifted[:rows - SUB * m]
                total = jnp.concatenate((total[:SUB * m], rest), axis=0) if m else rest
        direct[:, lanes] = total
        return carry

    def own_rows(p):
        lax.fori_loop(p * strips, (p + 1) * strips, own_strip, 0)

    def send_own(slot, p, device):
        return pltpu.make_async_remote_copy(
            src_ref=blocks.at[0, p], dst_ref=blocks.at[slot, p], send_sem=block_send.at[slot, p],
            recv_sem=block_recv.at[slot, p], **peer(t, device),
        )

    def pass_on(slot, p):
        odd = slot % 2
        return pltpu.make_async_remote_copy(
            src_ref=blocks.at[slot, p], dst_ref=blocks.at[slot + 2, p], send_sem=block_send.at[slot + 2, p],
            recv_sem=block_recv.at[slot + 2, p], **peer(t, odd * ahead + (1 - odd) * behind),
        )

    def chord(source, slot, p):
        return pltpu.make_async_remote_copy(
            src_ref=blocks.at[source, p], dst_ref=blocks.at[slot, p], send_sem=block_send.at[slot, p],
            recv_sem=block_recv.at[slot, p], **peer(t, across),
        )

    before[pl.ds(TAPS, SUB), :] = jnp.zeros((SUB, LANES), jnp.float32)

    def gates(p, carry):
        @pl.when(p + 1 < parts)
        def _():
            own_rows(p + 1)

        @pl.when(jnp.logical_not(is_first))
        def _():
            tail_copy(p).wait_recv()

        def one(s, carry):
            lanes = strip_of(p * strips + s)
            before[pl.ds(0, TAPS), :] = tail_in[p, :, strip_of(s)].astype(jnp.float32)
            total = direct[pl.ds(0, TAPS), lanes]
            for r in range(SUB):
                shifted = before[pl.ds(SUB - r, TAPS), :]
                for m in range(TAPS // SUB):
                    tap = long_ref[pl.ds(SUB * m + r, 1), lanes]
                    count = SUB * (m + 1)
                    head = total[:count] + tap * shifted[TAPS - count:]
                    total = jnp.concatenate((head, total[count:]), axis=0) if count < TAPS else head
            extend(lanes, (0,))
            gate = short(0, lanes, 0, rows)
            later = gate[TAPS:] * direct[pl.ds(TAPS, rows - TAPS), lanes]
            blocks[0, p, pl.ds(0, TAPS), strip_of(s)] = (gate[:TAPS] * total).astype(jnp.bfloat16)
            blocks[0, p, pl.ds(TAPS, rows - TAPS), strip_of(s)] = later.astype(jnp.bfloat16)
            return carry

        lax.fori_loop(0, strips, one, 0)
        send_own(1, p, ahead).start()
        send_own(2, p, behind).start()
        return carry

    own_rows(0)
    lax.fori_loop(0, parts, gates, 0)

    own_columns.wait()
    columns.wait_recv()

    def tp_copy(slot):
        return pltpu.make_async_remote_copy(
            src_ref=sent.at[slot], dst_ref=other.at[slot], send_sem=tp_send.at[slot], recv_sem=tp_recv.at[slot],
            **peer(1 - t, cp),
        )

    def out_copy(slot):
        odd, step = slot % 2, (slot + 1) // 2
        return pltpu.make_async_remote_copy(
            src_ref=summed.at[slot], dst_ref=landed.at[my_piece], send_sem=out_send.at[slot],
            recv_sem=out_recv.at[my_piece], **peer(half_owner, cp_at(place + (1 - 2 * odd) * forth * step)),
        )

    width = weights.shape[2]
    tile = min(256, width)

    def multiply(slot, p, first):
        depth_rows = pl.ds(pl.multiple_of(p * part, part), part)

        def one(j, carry):
            lanes = pl.ds(pl.multiple_of(j * tile, tile), tile)
            for side in range(2):
                value = jnp.dot(
                    blocks[slot, p], weights[side, depth_rows, lanes], preferred_element_type=jnp.float32
                )
                if not first:
                    value = value + totals[slot % 2, side, :, lanes]
                totals[slot % 2, side, :, lanes] = value
            return carry

        lax.fori_loop(0, width // tile, one, 0)

    def emit(slot):
        sent[slot] = totals[slot % 2, 1 - t].astype(jnp.bfloat16)
        tp_copy(slot).start()
        kept[slot] = totals[slot % 2, t].astype(jnp.bfloat16)

    def finish(slot):
        tp_copy(slot).wait_recv()
        total = (kept[slot].astype(jnp.float32) + other[slot].astype(jnp.float32)).astype(jnp.bfloat16)
        stays = jnp.logical_and(slot == 0, half_owner == t)

        @pl.when(stays)
        def _():
            landed[my_piece] = total

        @pl.when(jnp.logical_not(stays))
        def _():
            summed[slot] = total
            out_copy(slot).start()

    def take(slot, p, first):
        pltpu.make_async_copy(blocks.at[slot, p], blocks.at[slot, p], block_recv.at[slot, p]).wait()

        onward = slot + 2 < n
        onward = jnp.logical_and(onward, jnp.logical_not(jnp.logical_and(slot == n - 3, takes_sixth)))
        onward = jnp.logical_and(onward, jnp.logical_not(jnp.logical_and(slot == n - 4, takes_seventh)))

        @pl.when(onward)
        def _():
            pass_on(slot, p).start()

        @pl.when(jnp.logical_and(slot == 2, takes_sixth))
        def _():
            chord(2, n - 1, p).start()

        @pl.when(jnp.logical_and(slot == 3, takes_seventh))
        def _():
            chord(3, n - 2, p).start()

        multiply(slot, p, first)

    def take_last(p, first):
        pltpu.make_async_copy(blocks.at[n - 1, p], blocks.at[n - 1, p], block_recv.at[n - 1, p]).wait()
        multiply(n - 1, p, first)

    multiply(0, 0, True)
    lax.fori_loop(1, parts, lambda p, carry: (multiply(0, p, False), carry)[1], 0)
    emit(0)

    def pair(i, carry):
        odd, even = 2 * i - 1, 2 * i

        def both(p, first):
            take(odd, p, first)
            take(even, p, first)

        both(0, True)
        lax.fori_loop(1, parts, lambda p, carry: (both(p, False), carry)[1], 0)
        emit(odd)
        emit(even)
        finish(odd - 1)

        @pl.when(i > 1)
        def _():
            finish(odd - 2)

        return carry

    lax.fori_loop(1, depth, pair, 0)
    take_last(0, True)
    finish(n - 2)
    finish(n - 3)
    lax.fori_loop(1, parts, lambda p, carry: (take_last(p, False), carry)[1], 0)
    emit(n - 1)
    finish(n - 1)

    columns.wait_send()

    @pl.when(jnp.logical_not(is_last))
    def _():
        edge_copy.wait_send()

    def drain_parts(p, carry):
        @pl.when(jnp.logical_not(is_last))
        def _():
            tail_copy(p).wait_send()

        send_own(1, p, ahead).wait_send()
        send_own(2, p, behind).wait_send()
        lax.fori_loop(1, n - 2, lambda slot, carry: (pass_on(slot, p).wait_send(), carry)[1], 0)
        return carry

    lax.fori_loop(0, parts, drain_parts, 0)

    def drain(slot, carry):
        tp_copy(slot).wait_send()

        @pl.when(jnp.logical_not(jnp.logical_and(slot == 0, half_owner == t)))
        def _():
            out_copy(slot).wait_send()

        return carry

    lax.fori_loop(0, n, drain, 0)
    for piece in range(n):
        @pl.when(jnp.logical_not(jnp.logical_and(piece == my_piece, half_owner == t)))
        def _():
            pltpu.make_async_copy(landed.at[piece], landed.at[piece], out_recv.at[piece]).wait()

        out_ref[:, pl.ds(piece * width, width)] = landed[piece]


def mixer(features, short_filter, long_filter, skip_scale, out_weight, n):
    _, rows, channels = features.shape
    width = out_weight.shape[1]
    parts = 4
    part = channels // parts
    kind = jnp.bfloat16
    dma = pltpu.SemaphoreType.DMA
    whole = pl.BlockSpec(memory_space=pltpu.VMEM)
    return pl.pallas_call(
        functools.partial(mixer_kernel, n, parts),
        out_shape=jax.ShapeDtypeStruct((rows, n * width), kind),
        in_specs=[whole] * 4 + [pl.BlockSpec(memory_space=pl.ANY)],
        out_specs=whole,
        scratch_shapes=[
            pltpu.VMEM((n, parts, rows, part), kind),
            pltpu.VMEM((2, channels, width), kind),
            *[pltpu.VMEM((n, rows, width), kind)] * 5,
            pltpu.VMEM((2, 2, rows, width), jnp.float32),
            pltpu.VMEM((rows, channels), jnp.float32),
            *[pltpu.VMEM((2 * SUB, channels), kind)] * 2,
            *[pltpu.VMEM((parts, TAPS, part), kind)] * 2,
            pltpu.VMEM((3, SUB + rows, LANES), jnp.float32),
            pltpu.VMEM((SUB + rows, LANES), jnp.float32),
            pltpu.VMEM((TAPS + SUB, LANES), jnp.float32),
            dma, dma((2,)), dma((parts,)), dma((parts,)), dma((n, parts)), dma((n, parts)), dma, dma,
            dma((n,)), dma((n,)), dma((n,)), dma((n,)),
        ],
        compiler_params=pltpu.CompilerParams(
            collective_id=0, has_side_effects=True, vmem_limit_bytes=56 * 2**20
        ),
        cost_estimate=pl.CostEstimate(
            flops=4 * n * rows * channels * width, bytes_accessed=4 * channels * width, transcendentals=0
        ),
        name="mixer",
    )(features, short_filter, long_filter, skip_scale.reshape(1, channels), out_weight)


def local(on_ring, features, short_filter, long_filter, skip_scale, out_weight):
    rows = features.shape[1]
    if on_ring:
        return mixer(features, short_filter, long_filter, skip_scale, out_weight, lax.axis_size("cp") // 2)
    product, edge = halo_of(features, short_filter)
    halo = from_behind(product, "cp", 1)
    edge = from_behind(edge, "cp", 1)
    gated = gate_conv(features, halo, edge, short_filter, long_filter, skip_scale, rows)
    everyone = lax.all_gather(gated, "cp", axis=0, tiled=True)
    partial_value = jnp.dot(everyone, out_weight, preferred_element_type=jnp.float32).astype(jnp.bfloat16)
    mine = lax.all_to_all(partial_value, "cp", split_axis=0, concat_axis=1, tiled=True)
    return lax.psum_scatter(mine, "tp", scatter_dimension=1, tiled=True)


def solution(mesh):
    on_ring = mesh.shape["tp"] == 2 and mesh.shape["cp"] == 16
    return jax.shard_map(
        functools.partial(local, on_ring),
        mesh=mesh,
        in_specs=(P(None, "cp", "tp"), P(None, None, "tp"), P(None, "tp"), P("tp"), P("tp", "cp")),
        out_specs=P("cp", "tp"),
        check_vma=False,
    )
```

```python
import functools

import jax
import jax.numpy as jnp
from jax import lax
from jax.experimental import pallas as pl
from jax.experimental.pallas import tpu as pltpu
from jax.sharding import PartitionSpec as P

TAPS = 128
SHORT = 3
LANES = 128
SUB = 8


def from_behind(block, axis, distance):
    devices = range(lax.axis_size(axis))
    route = [(i - distance, i) for i in devices if i - distance in devices]
    return lax.ppermute(block, axis, route)


def conv_kernel(rows, width, feat_ref, halo_ref, edge_ref, short_ref, long_ref, skip_ref, out_ref, ext, prod):
    def strip(index, carry):
        lanes = pl.ds(pl.multiple_of(index * LANES, LANES), LANES)
        shorted = []
        for i in range(3):
            ext[i, pl.ds(0, SUB), :] = edge_ref[i, :, lanes].astype(jnp.float32)
            ext[i, pl.ds(SUB, rows), :] = feat_ref[i, :, lanes].astype(jnp.float32)
            total = short_ref[i, pl.ds(0, 1), lanes] * ext[i, pl.ds(SUB, rows), :]
            for lag in range(1, SHORT):
                total = total + short_ref[i, pl.ds(lag, 1), lanes] * ext[i, pl.ds(SUB - lag, rows), :]
            shorted.append(total)
        product = shorted[1] * shorted[2]
        prod[pl.ds(0, TAPS), :] = halo_ref[:, lanes].astype(jnp.float32)
        prod[pl.ds(TAPS, rows), :] = product
        total = skip_ref[:, lanes] * product
        span = rows + TAPS - SUB
        for r in range(SUB):
            shifted = prod[pl.ds(SUB - r, span), :]
            for m in range(TAPS // SUB):
                begin = TAPS - SUB - SUB * m
                total = total + long_ref[pl.ds(SUB * m + r, 1), lanes] * shifted[begin:begin + rows]
        out_ref[pl.ds(0, rows), lanes] = (shorted[0] * total).astype(jnp.bfloat16)
        if out_ref.shape[0] > rows:
            out_ref[pl.ds(rows, out_ref.shape[0] - rows), lanes] = jnp.zeros(
                (out_ref.shape[0] - rows, LANES), jnp.bfloat16
            )
        return carry

    lax.fori_loop(0, width // LANES, strip, 0)


def gate_conv(features, halo, edge, short_filter, long_filter, skip_scale, out_rows):
    _, rows, channels = features.shape
    width = min(512, channels)
    return pl.pallas_call(
        functools.partial(conv_kernel, rows, width),
        grid=(channels // width,),
        out_shape=jax.ShapeDtypeStruct((out_rows, channels), jnp.bfloat16),
        in_specs=[
            pl.BlockSpec((3, rows, width), lambda c: (0, 0, c)),
            pl.BlockSpec((TAPS, width), lambda c: (0, c)),
            pl.BlockSpec((3, SUB, width), lambda c: (0, 0, c)),
            pl.BlockSpec((3, SHORT, width), lambda c: (0, 0, c)),
            pl.BlockSpec((TAPS, width), lambda c: (0, c)),
            pl.BlockSpec((1, width), lambda c: (0, c)),
        ],
        out_specs=pl.BlockSpec((out_rows, width), lambda c: (0, c)),
        scratch_shapes=[
            pltpu.VMEM((3, SUB + rows, LANES), jnp.float32),
            pltpu.VMEM((TAPS + rows, LANES), jnp.float32),
        ],
        compiler_params=pltpu.CompilerParams(vmem_limit_bytes=32 * 2**20),
        cost_estimate=pl.CostEstimate(
            flops=2 * TAPS * rows * channels, bytes_accessed=10 * rows * channels, transcendentals=0
        ),
        name="gate_conv",
    )(features, halo, edge, short_filter, long_filter, skip_scale.reshape(1, channels))


def halo_of(features, short_filter):
    rows = features.shape[1]
    tail = features[1:, rows - TAPS - SHORT + 1:, :].astype(jnp.float32)
    shorted = sum(
        short_filter[1:, lag, None, :] * tail[:, SHORT - 1 - lag:SHORT - 1 - lag + TAPS] for lag in range(SHORT)
    )
    product = (shorted[0] * shorted[1]).astype(jnp.bfloat16)
    return product, features[:, rows - SUB:, :]


def mixer_kernel(
    n, parts, feat_ref, short_ref, long_ref, skip_ref, weight_ref, out_ref,
    blocks, weights, kept, sent, other, summed, landed, totals, direct, edge_out, edge_in, tail_out, tail_in, ext, prod, before,
    own_sem, edge_sem, tail_send, tail_recv, block_send, block_recv, weight_send, weight_recv,
    tp_send, tp_recv, out_send, out_recv,
):
    t, cp = lax.axis_index("tp"), lax.axis_index("cp")
    rows = feat_ref.shape[1]
    part = blocks.shape[3]
    core, chip = cp % 2, cp // 2
    x, z = chip % 2, chip // 2
    depth = n // 2
    place = x * (n - 1 - z) + (1 - x) * z
    forth = 1 - 2 * core
    half_owner = chip // depth
    my_piece = (chip % depth) * 2 + t

    def cp_at(ring_place):
        r = (ring_place + 2 * n) % n
        rx = r // depth
        rz = rx * (n - 1 - r) + (1 - rx) * r
        return (rz * 2 + rx) * 2 + core

    def peer(a, b):
        return dict(device_id=(a, b), device_id_type=pl.DeviceIdType.MESH)

    ahead, behind = cp_at(place + forth), cp_at(place - forth)
    sibling = cp + 1 - 2 * core
    across = cp_at(n - 1 - place)
    takes_seventh, takes_sixth = place % depth == 2 - core, place % depth == 1 + core
    is_first, is_last = cp == 0, cp == 2 * n - 1

    barrier = pltpu.get_barrier_semaphore()
    for device in ((t, ahead), (t, behind), (t, sibling), (1 - t, cp)):
        pl.semaphore_signal(barrier, inc=1, **peer(*device))

    @pl.when(jnp.logical_or(takes_seventh, takes_sixth))
    def _():
        pl.semaphore_signal(barrier, inc=1, **peer(t, across))

    @pl.when(cp > 0)
    def _():
        pl.semaphore_signal(barrier, inc=1, **peer(t, cp - 1))

    def greet(i, carry):
        sender = (t * depth + i // 2) * 2 + core

        @pl.when(jnp.logical_or(i % 2 != t, sender != cp))
        def _():
            pl.semaphore_signal(barrier, inc=1, **peer(i % 2, sender))

        return carry

    lax.fori_loop(0, n, greet, 0)
    has_chord, has_next = (place % depth + 1) // 2 % 2, (4 * n - 3 - cp) // (2 * n - 1)

    columns = pltpu.make_async_remote_copy(
        src_ref=weight_ref, dst_ref=weights.at[core], send_sem=weight_send, recv_sem=weight_recv, **peer(t, sibling)
    )
    own_columns = pltpu.make_async_copy(weight_ref, weights.at[core], own_sem)
    edge_copy = pltpu.make_async_remote_copy(
        src_ref=edge_out, dst_ref=edge_in, send_sem=edge_sem.at[0], recv_sem=edge_sem.at[1], **peer(t, cp + 1)
    )

    def tail_copy(p):
        return pltpu.make_async_remote_copy(
            src_ref=tail_out.at[p], dst_ref=tail_in.at[p], send_sem=tail_send.at[p], recv_sem=tail_recv.at[p],
            **peer(t, cp + 1),
        )

    def strip_of(index):
        return pl.ds(pl.multiple_of(index * LANES, LANES), LANES)

    strips = part // LANES

    def edges(index, carry):
        lanes = strip_of(index)
        q, k, v = (feat_ref[i, pl.ds(rows - SUB, SUB), lanes].astype(jnp.float32) for i in range(3))
        row = lax.broadcasted_iota(jnp.int32, (SUB, LANES), 0)
        kv = jnp.where(row >= SUB - 2, k, pltpu.roll(v, SUB - 2, 0))
        edge_out[:, lanes] = jnp.concatenate((q, kv), axis=0).astype(jnp.bfloat16)
        return carry

    lax.fori_loop(0, parts * strips, edges, 0)

    def short(i, lanes, begin, count):
        total = short_ref[i, pl.ds(0, 1), lanes] * ext[i, pl.ds(SUB + begin, count), :]
        for lag in range(1, SHORT):
            total = total + short_ref[i, pl.ds(lag, 1), lanes] * ext[i, pl.ds(SUB + begin - lag, count), :]
        return total

    def tails(p):
        def one(s, carry):
            lanes = strip_of(p * strips + s)
            for i in (1, 2):
                ext[i, pl.ds(SUB, rows), :] = feat_ref[i, :, lanes].astype(jnp.float32)
            product = short(1, lanes, rows - TAPS, TAPS) * short(2, lanes, rows - TAPS, TAPS)
            tail_out[p, :, strip_of(s)] = product.astype(jnp.bfloat16)
            return carry

        lax.fori_loop(0, strips, one, 0)

    def send_tail(p):
        @pl.when(jnp.logical_not(is_last))
        def _():
            tail_copy(p).start()

    tails(0)
    pl.semaphore_wait(barrier, 4 + n - 1 + (half_owner + t) % 2 + has_chord + has_next)

    @pl.when(jnp.logical_not(is_last))
    def _():
        edge_copy.start()

    send_tail(0)
    own_columns.start()
    lax.fori_loop(1, parts, lambda p, carry: (tails(p), send_tail(p), carry)[2], 0)
    columns.start()

    @pl.when(is_first)
    def _():
        edge_in[...] = jnp.zeros_like(edge_in)
        tail_in[...] = jnp.zeros_like(tail_in)

    @pl.when(jnp.logical_not(is_first))
    def _():
        edge_copy.wait_recv()

    def extend(lanes, which):
        edge = edge_in[:, lanes].astype(jnp.float32)
        q, kv = edge[:SUB], edge[SUB:]
        ahead_rows = (q, kv, pltpu.roll(kv, 2, 0))
        for i in which:
            ext[i, pl.ds(0, SUB), :] = ahead_rows[i]
            ext[i, pl.ds(SUB, rows), :] = feat_ref[i, :, lanes].astype(jnp.float32)

    prod[pl.ds(0, SUB), :] = jnp.zeros((SUB, LANES), jnp.float32)

    def own_strip(index, carry):
        lanes = strip_of(index)
        extend(lanes, (1, 2))
        product = short(1, lanes, 0, rows) * short(2, lanes, 0, rows)
        prod[pl.ds(SUB, rows), :] = product
        total = skip_ref[:, lanes] * product
        for r in range(SUB):
            shifted = prod[pl.ds(SUB - r, rows), :]
            for m in range(TAPS // SUB):
                tap = long_ref[pl.ds(SUB * m + r, 1), lanes]
                rest = total[SUB * m:] + tap * shifted[:rows - SUB * m]
                total = jnp.concatenate((total[:SUB * m], rest), axis=0) if m else rest
        direct[:, lanes] = total
        return carry

    def own_rows(p):
        lax.fori_loop(p * strips, (p + 1) * strips, own_strip, 0)

    def send_own(slot, p, device):
        return pltpu.make_async_remote_copy(
            src_ref=blocks.at[0, p], dst_ref=blocks.at[slot, p], send_sem=block_send.at[slot, p],
            recv_sem=block_recv.at[slot, p], **peer(t, device),
        )

    def pass_on(slot, p):
        odd = slot % 2
        return pltpu.make_async_remote_copy(
            src_ref=blocks.at[slot, p], dst_ref=blocks.at[slot + 2, p], send_sem=block_send.at[slot + 2, p],
            recv_sem=block_recv.at[slot + 2, p], **peer(t, odd * ahead + (1 - odd) * behind),
        )

    def chord(source, slot, p):
        return pltpu.make_async_remote_copy(
            src_ref=blocks.at[source, p], dst_ref=blocks.at[slot, p], send_sem=block_send.at[slot, p],
            recv_sem=block_recv.at[slot, p], **peer(t, across),
        )

    before[pl.ds(TAPS, SUB), :] = jnp.zeros((SUB, LANES), jnp.float32)

    def gates(p, carry):
        own_rows(p)

        @pl.when(jnp.logical_not(is_first))
        def _():
            tail_copy(p).wait_recv()

        def one(s, carry):
            lanes = strip_of(p * strips + s)
            before[pl.ds(0, TAPS), :] = tail_in[p, :, strip_of(s)].astype(jnp.float32)
            total = direct[pl.ds(0, TAPS), lanes]
            for r in range(SUB):
                shifted = before[pl.ds(SUB - r, TAPS), :]
                for m in range(TAPS // SUB):
                    tap = long_ref[pl.ds(SUB * m + r, 1), lanes]
                    count = SUB * (m + 1)
                    head = total[:count] + tap * shifted[TAPS - count:]
                    total = jnp.concatenate((head, total[count:]), axis=0) if count < TAPS else head
            extend(lanes, (0,))
            gate = short(0, lanes, 0, rows)
            later = gate[TAPS:] * direct[pl.ds(TAPS, rows - TAPS), lanes]
            blocks[0, p, pl.ds(0, TAPS), strip_of(s)] = (gate[:TAPS] * total).astype(jnp.bfloat16)
            blocks[0, p, pl.ds(TAPS, rows - TAPS), strip_of(s)] = later.astype(jnp.bfloat16)
            return carry

        lax.fori_loop(0, strips, one, 0)
        send_own(1, p, ahead).start()
        send_own(2, p, behind).start()
        return carry

    lax.fori_loop(0, parts, gates, 0)

    own_columns.wait()
    columns.wait_recv()

    def tp_copy(slot):
        return pltpu.make_async_remote_copy(
            src_ref=sent.at[slot], dst_ref=other.at[slot], send_sem=tp_send.at[slot], recv_sem=tp_recv.at[slot],
            **peer(1 - t, cp),
        )

    def out_copy(slot):
        odd, step = slot % 2, (slot + 1) // 2
        return pltpu.make_async_remote_copy(
            src_ref=summed.at[slot], dst_ref=landed.at[my_piece], send_sem=out_send.at[slot],
            recv_sem=out_recv.at[my_piece], **peer(half_owner, cp_at(place + (1 - 2 * odd) * forth * step)),
        )

    width = weights.shape[2]
    tile = min(256, width)

    def multiply(slot, p, first):
        depth_rows = pl.ds(pl.multiple_of(p * part, part), part)

        def one(j, carry):
            lanes = pl.ds(pl.multiple_of(j * tile, tile), tile)
            for side in range(2):
                value = jnp.dot(
                    blocks[slot, p], weights[side, depth_rows, lanes], preferred_element_type=jnp.float32
                )
                if not first:
                    value = value + totals[slot % 2, side, :, lanes]
                totals[slot % 2, side, :, lanes] = value
            return carry

        lax.fori_loop(0, width // tile, one, 0)

    def emit(slot):
        sent[slot] = totals[slot % 2, 1 - t].astype(jnp.bfloat16)
        tp_copy(slot).start()
        kept[slot] = totals[slot % 2, t].astype(jnp.bfloat16)

    def finish(slot):
        tp_copy(slot).wait_recv()
        total = (kept[slot].astype(jnp.float32) + other[slot].astype(jnp.float32)).astype(jnp.bfloat16)
        stays = jnp.logical_and(slot == 0, half_owner == t)

        @pl.when(stays)
        def _():
            landed[my_piece] = total

        @pl.when(jnp.logical_not(stays))
        def _():
            summed[slot] = total
            out_copy(slot).start()

    def take(slot, p, first):
        pltpu.make_async_copy(blocks.at[slot, p], blocks.at[slot, p], block_recv.at[slot, p]).wait()

        onward = slot + 2 < n
        onward = jnp.logical_and(onward, jnp.logical_not(jnp.logical_and(slot == n - 3, takes_sixth)))
        onward = jnp.logical_and(onward, jnp.logical_not(jnp.logical_and(slot == n - 4, takes_seventh)))

        @pl.when(onward)
        def _():
            pass_on(slot, p).start()

        @pl.when(jnp.logical_and(slot == 2, takes_sixth))
        def _():
            chord(2, n - 1, p).start()

        @pl.when(jnp.logical_and(slot == 3, takes_seventh))
        def _():
            chord(3, n - 2, p).start()

        multiply(slot, p, first)

    def take_last(p, first):
        pltpu.make_async_copy(blocks.at[n - 1, p], blocks.at[n - 1, p], block_recv.at[n - 1, p]).wait()
        multiply(n - 1, p, first)

    multiply(0, 0, True)
    lax.fori_loop(1, parts, lambda p, carry: (multiply(0, p, False), carry)[1], 0)
    emit(0)

    def pair(i, carry):
        odd, even = 2 * i - 1, 2 * i

        def both(p, first):
            take(odd, p, first)
            take(even, p, first)

        both(0, True)
        finish(odd - 1)

        @pl.when(i > 1)
        def _():
            finish(odd - 2)

        lax.fori_loop(1, parts, lambda p, carry: (both(p, False), carry)[1], 0)
        emit(odd)
        emit(even)
        return carry

    lax.fori_loop(1, depth, pair, 0)
    take_last(0, True)
    finish(n - 2)
    finish(n - 3)
    lax.fori_loop(1, parts, lambda p, carry: (take_last(p, False), carry)[1], 0)
    emit(n - 1)
    finish(n - 1)

    for piece in range(n):
        @pl.when(jnp.logical_not(jnp.logical_and(piece == my_piece, half_owner == t)))
        def _():
            pltpu.make_async_copy(landed.at[piece], landed.at[piece], out_recv.at[piece]).wait()

        out_ref[:, pl.ds(piece * width, width)] = landed[piece]

    columns.wait_send()

    @pl.when(jnp.logical_not(is_last))
    def _():
        edge_copy.wait_send()

    def drain_parts(p, carry):
        @pl.when(jnp.logical_not(is_last))
        def _():
            tail_copy(p).wait_send()

        send_own(1, p, ahead).wait_send()
        send_own(2, p, behind).wait_send()
        lax.fori_loop(1, n - 2, lambda slot, carry: (pass_on(slot, p).wait_send(), carry)[1], 0)
        return carry

    lax.fori_loop(0, parts, drain_parts, 0)

    def drain(slot, carry):
        tp_copy(slot).wait_send()

        @pl.when(jnp.logical_not(jnp.logical_and(slot == 0, half_owner == t)))
        def _():
            out_copy(slot).wait_send()

        return carry

    lax.fori_loop(0, n, drain, 0)


def mixer(features, short_filter, long_filter, skip_scale, out_weight, n):
    _, rows, channels = features.shape
    width = out_weight.shape[1]
    parts = 8
    part = channels // parts
    kind = jnp.bfloat16
    dma = pltpu.SemaphoreType.DMA
    whole = pl.BlockSpec(memory_space=pltpu.VMEM)
    return pl.pallas_call(
        functools.partial(mixer_kernel, n, parts),
        out_shape=jax.ShapeDtypeStruct((rows, n * width), kind),
        in_specs=[whole] * 4 + [pl.BlockSpec(memory_space=pl.ANY)],
        out_specs=whole,
        scratch_shapes=[
            pltpu.VMEM((n, parts, rows, part), kind),
            pltpu.VMEM((2, channels, width), kind),
            *[pltpu.VMEM((n, rows, width), kind)] * 5,
            pltpu.VMEM((2, 2, rows, width), jnp.float32),
            pltpu.VMEM((rows, channels), jnp.float32),
            *[pltpu.VMEM((2 * SUB, channels), kind)] * 2,
            *[pltpu.VMEM((parts, TAPS, part), kind)] * 2,
            pltpu.VMEM((3, SUB + rows, LANES), jnp.float32),
            pltpu.VMEM((SUB + rows, LANES), jnp.float32),
            pltpu.VMEM((TAPS + SUB, LANES), jnp.float32),
            dma, dma((2,)), dma((parts,)), dma((parts,)), dma((n, parts)), dma((n, parts)), dma, dma,
            dma((n,)), dma((n,)), dma((n,)), dma((n,)),
        ],
        compiler_params=pltpu.CompilerParams(
            collective_id=0, has_side_effects=True, vmem_limit_bytes=56 * 2**20
        ),
        cost_estimate=pl.CostEstimate(
            flops=4 * n * rows * channels * width, bytes_accessed=4 * channels * width, transcendentals=0
        ),
        name="mixer",
    )(features, short_filter, long_filter, skip_scale.reshape(1, channels), out_weight)


def local(on_ring, features, short_filter, long_filter, skip_scale, out_weight):
    rows = features.shape[1]
    if on_ring:
        return mixer(features, short_filter, long_filter, skip_scale, out_weight, lax.axis_size("cp") // 2)
    product, edge = halo_of(features, short_filter)
    halo = from_behind(product, "cp", 1)
    edge = from_behind(edge, "cp", 1)
    gated = gate_conv(features, halo, edge, short_filter, long_filter, skip_scale, rows)
    everyone = lax.all_gather(gated, "cp", axis=0, tiled=True)
    partial_value = jnp.dot(everyone, out_weight, preferred_element_type=jnp.float32).astype(jnp.bfloat16)
    mine = lax.all_to_all(partial_value, "cp", split_axis=0, concat_axis=1, tiled=True)
    return lax.psum_scatter(mine, "tp", scatter_dimension=1, tiled=True)


def solution(mesh):
    on_ring = mesh.shape["tp"] == 2 and mesh.shape["cp"] == 16
    return jax.shard_map(
        functools.partial(local, on_ring),
        mesh=mesh,
        in_specs=(P(None, "cp", "tp"), P(None, None, "tp"), P(None, "tp"), P("tp"), P("tp", "cp")),
        out_specs=P("cp", "tp"),
        check_vma=False,
    )
```

```python
import functools

import jax
import jax.numpy as jnp
from jax import lax
from jax.experimental import pallas as pl
from jax.experimental.pallas import tpu as pltpu
from jax.sharding import PartitionSpec as P

TAPS = 128
SHORT = 3
LANES = 128
SUB = 8


def from_behind(block, axis, distance):
    devices = range(lax.axis_size(axis))
    route = [(i - distance, i) for i in devices if i - distance in devices]
    return lax.ppermute(block, axis, route)


def conv_kernel(rows, width, feat_ref, halo_ref, edge_ref, short_ref, long_ref, skip_ref, out_ref, ext, prod):
    def strip(index, carry):
        lanes = pl.ds(pl.multiple_of(index * LANES, LANES), LANES)
        shorted = []
        for i in range(3):
            ext[i, pl.ds(0, SUB), :] = edge_ref[i, :, lanes].astype(jnp.float32)
            ext[i, pl.ds(SUB, rows), :] = feat_ref[i, :, lanes].astype(jnp.float32)
            total = short_ref[i, pl.ds(0, 1), lanes] * ext[i, pl.ds(SUB, rows), :]
            for lag in range(1, SHORT):
                total = total + short_ref[i, pl.ds(lag, 1), lanes] * ext[i, pl.ds(SUB - lag, rows), :]
            shorted.append(total)
        product = shorted[1] * shorted[2]
        prod[pl.ds(0, TAPS), :] = halo_ref[:, lanes].astype(jnp.float32)
        prod[pl.ds(TAPS, rows), :] = product
        total = skip_ref[:, lanes] * product
        span = rows + TAPS - SUB
        for r in range(SUB):
            shifted = prod[pl.ds(SUB - r, span), :]
            for m in range(TAPS // SUB):
                begin = TAPS - SUB - SUB * m
                total = total + long_ref[pl.ds(SUB * m + r, 1), lanes] * shifted[begin:begin + rows]
        out_ref[pl.ds(0, rows), lanes] = (shorted[0] * total).astype(jnp.bfloat16)
        if out_ref.shape[0] > rows:
            out_ref[pl.ds(rows, out_ref.shape[0] - rows), lanes] = jnp.zeros(
                (out_ref.shape[0] - rows, LANES), jnp.bfloat16
            )
        return carry

    lax.fori_loop(0, width // LANES, strip, 0)


def gate_conv(features, halo, edge, short_filter, long_filter, skip_scale, out_rows):
    _, rows, channels = features.shape
    width = min(512, channels)
    return pl.pallas_call(
        functools.partial(conv_kernel, rows, width),
        grid=(channels // width,),
        out_shape=jax.ShapeDtypeStruct((out_rows, channels), jnp.bfloat16),
        in_specs=[
            pl.BlockSpec((3, rows, width), lambda c: (0, 0, c)),
            pl.BlockSpec((TAPS, width), lambda c: (0, c)),
            pl.BlockSpec((3, SUB, width), lambda c: (0, 0, c)),
            pl.BlockSpec((3, SHORT, width), lambda c: (0, 0, c)),
            pl.BlockSpec((TAPS, width), lambda c: (0, c)),
            pl.BlockSpec((1, width), lambda c: (0, c)),
        ],
        out_specs=pl.BlockSpec((out_rows, width), lambda c: (0, c)),
        scratch_shapes=[
            pltpu.VMEM((3, SUB + rows, LANES), jnp.float32),
            pltpu.VMEM((TAPS + rows, LANES), jnp.float32),
        ],
        compiler_params=pltpu.CompilerParams(vmem_limit_bytes=32 * 2**20),
        cost_estimate=pl.CostEstimate(
            flops=2 * TAPS * rows * channels, bytes_accessed=10 * rows * channels, transcendentals=0
        ),
        name="gate_conv",
    )(features, halo, edge, short_filter, long_filter, skip_scale.reshape(1, channels))


def halo_of(features, short_filter):
    rows = features.shape[1]
    tail = features[1:, rows - TAPS - SHORT + 1:, :].astype(jnp.float32)
    shorted = sum(
        short_filter[1:, lag, None, :] * tail[:, SHORT - 1 - lag:SHORT - 1 - lag + TAPS] for lag in range(SHORT)
    )
    product = (shorted[0] * shorted[1]).astype(jnp.bfloat16)
    return product, features[:, rows - SUB:, :]


def mixer_kernel(
    n, parts, feat_ref, short_ref, long_ref, skip_ref, weight_ref, out_ref,
    blocks, weights, kept, sent, other, summed, landed, totals, direct, edge_out, edge_in, tail_out, tail_in, ext, prod, before,
    own_sem, edge_sem, tail_send, tail_recv, block_send, block_recv, weight_send, weight_recv,
    tp_send, tp_recv, out_send, out_recv,
):
    t, cp = lax.axis_index("tp"), lax.axis_index("cp")
    rows = feat_ref.shape[1]
    part = blocks.shape[3]
    core, chip = cp % 2, cp // 2
    x, z = chip % 2, chip // 2
    depth = n // 2
    place = x * (n - 1 - z) + (1 - x) * z
    forth = 1 - 2 * core
    half_owner = chip // depth
    my_piece = (chip % depth) * 2 + t

    def cp_at(ring_place):
        r = (ring_place + 2 * n) % n
        rx = r // depth
        rz = rx * (n - 1 - r) + (1 - rx) * r
        return (rz * 2 + rx) * 2 + core

    def peer(a, b):
        return dict(device_id=(a, b), device_id_type=pl.DeviceIdType.MESH)

    ahead, behind = cp_at(place + forth), cp_at(place - forth)
    sibling = cp + 1 - 2 * core
    across = cp_at(n - 1 - place)
    takes_seventh, takes_sixth = place % depth == 2 - core, place % depth == 1 + core
    is_first, is_last = cp == 0, cp == 2 * n - 1

    barrier = pltpu.get_barrier_semaphore()
    for device in ((t, ahead), (t, behind), (t, sibling), (1 - t, cp)):
        pl.semaphore_signal(barrier, inc=1, **peer(*device))

    @pl.when(jnp.logical_or(takes_seventh, takes_sixth))
    def _():
        pl.semaphore_signal(barrier, inc=1, **peer(t, across))

    @pl.when(cp > 0)
    def _():
        pl.semaphore_signal(barrier, inc=1, **peer(t, cp - 1))

    def greet(i, carry):
        sender = (t * depth + i // 2) * 2 + core

        @pl.when(jnp.logical_or(i % 2 != t, sender != cp))
        def _():
            pl.semaphore_signal(barrier, inc=1, **peer(i % 2, sender))

        return carry

    lax.fori_loop(0, n, greet, 0)
    has_chord, has_next = (place % depth + 1) // 2 % 2, (4 * n - 3 - cp) // (2 * n - 1)

    columns = pltpu.make_async_remote_copy(
        src_ref=weight_ref, dst_ref=weights.at[core], send_sem=weight_send, recv_sem=weight_recv, **peer(t, sibling)
    )
    own_columns = pltpu.make_async_copy(weight_ref, weights.at[core], own_sem)
    edge_copy = pltpu.make_async_remote_copy(
        src_ref=edge_out, dst_ref=edge_in, send_sem=edge_sem.at[0], recv_sem=edge_sem.at[1], **peer(t, cp + 1)
    )

    def tail_copy(p):
        return pltpu.make_async_remote_copy(
            src_ref=tail_out.at[p], dst_ref=tail_in.at[p], send_sem=tail_send.at[p], recv_sem=tail_recv.at[p],
            **peer(t, cp + 1),
        )

    def strip_of(index):
        return pl.ds(pl.multiple_of(index * LANES, LANES), LANES)

    strips = part // LANES

    def edges(index, carry):
        lanes = strip_of(index)
        q, k, v = (feat_ref[i, pl.ds(rows - SUB, SUB), lanes].astype(jnp.float32) for i in range(3))
        row = lax.broadcasted_iota(jnp.int32, (SUB, LANES), 0)
        kv = jnp.where(row >= SUB - 2, k, pltpu.roll(v, SUB - 2, 0))
        edge_out[:, lanes] = jnp.concatenate((q, kv), axis=0).astype(jnp.bfloat16)
        return carry

    lax.fori_loop(0, parts * strips, edges, 0)

    def short(i, lanes, begin, count):
        total = short_ref[i, pl.ds(0, 1), lanes] * ext[i, pl.ds(SUB + begin, count), :]
        for lag in range(1, SHORT):
            total = total + short_ref[i, pl.ds(lag, 1), lanes] * ext[i, pl.ds(SUB + begin - lag, count), :]
        return total

    def tails(p):
        def one(s, carry):
            lanes = strip_of(p * strips + s)
            for i in (1, 2):
                ext[i, pl.ds(SUB, rows), :] = feat_ref[i, :, lanes].astype(jnp.float32)
            product = short(1, lanes, rows - TAPS, TAPS) * short(2, lanes, rows - TAPS, TAPS)
            tail_out[p, :, strip_of(s)] = product.astype(jnp.bfloat16)
            return carry

        lax.fori_loop(0, strips, one, 0)

    def send_tail(p):
        @pl.when(jnp.logical_not(is_last))
        def _():
            tail_copy(p).start()

    tails(0)
    pl.semaphore_wait(barrier, 4 + n - 1 + (half_owner + t) % 2 + has_chord + has_next)

    @pl.when(jnp.logical_not(is_last))
    def _():
        edge_copy.start()

    send_tail(0)
    own_columns.start()
    lax.fori_loop(1, parts, lambda p, carry: (tails(p), send_tail(p), carry)[2], 0)
    columns.start()

    @pl.when(is_first)
    def _():
        edge_in[...] = jnp.zeros_like(edge_in)
        tail_in[...] = jnp.zeros_like(tail_in)

    @pl.when(jnp.logical_not(is_first))
    def _():
        edge_copy.wait_recv()

    def extend(lanes, which):
        edge = edge_in[:, lanes].astype(jnp.float32)
        q, kv = edge[:SUB], edge[SUB:]
        ahead_rows = (q, kv, pltpu.roll(kv, 2, 0))
        for i in which:
            ext[i, pl.ds(0, SUB), :] = ahead_rows[i]
            ext[i, pl.ds(SUB, rows), :] = feat_ref[i, :, lanes].astype(jnp.float32)

    prod[pl.ds(0, SUB), :] = jnp.zeros((SUB, LANES), jnp.float32)

    def own_strip(index, carry):
        lanes = strip_of(index)
        extend(lanes, (1, 2))
        product = short(1, lanes, 0, rows) * short(2, lanes, 0, rows)
        prod[pl.ds(SUB, rows), :] = product
        total = skip_ref[:, lanes] * product
        for r in range(SUB):
            shifted = prod[pl.ds(SUB - r, rows), :]
            for m in range(TAPS // SUB):
                tap = long_ref[pl.ds(SUB * m + r, 1), lanes]
                rest = total[SUB * m:] + tap * shifted[:rows - SUB * m]
                total = jnp.concatenate((total[:SUB * m], rest), axis=0) if m else rest
        direct[:, lanes] = total
        return carry

    def own_rows(p):
        lax.fori_loop(p * strips, (p + 1) * strips, own_strip, 0)

    def send_own(slot, p, device):
        return pltpu.make_async_remote_copy(
            src_ref=blocks.at[0, p], dst_ref=blocks.at[slot, p], send_sem=block_send.at[slot, p],
            recv_sem=block_recv.at[slot, p], **peer(t, device),
        )

    def pass_on(slot, p):
        odd = slot % 2
        return pltpu.make_async_remote_copy(
            src_ref=blocks.at[slot, p], dst_ref=blocks.at[slot + 2, p], send_sem=block_send.at[slot + 2, p],
            recv_sem=block_recv.at[slot + 2, p], **peer(t, odd * ahead + (1 - odd) * behind),
        )

    def chord(source, slot, p):
        return pltpu.make_async_remote_copy(
            src_ref=blocks.at[source, p], dst_ref=blocks.at[slot, p], send_sem=block_send.at[slot, p],
            recv_sem=block_recv.at[slot, p], **peer(t, across),
        )

    before[pl.ds(TAPS, SUB), :] = jnp.zeros((SUB, LANES), jnp.float32)

    def gates(p, carry):
        own_rows(p)

        @pl.when(jnp.logical_not(is_first))
        def _():
            tail_copy(p).wait_recv()

        def one(s, carry):
            lanes = strip_of(p * strips + s)
            before[pl.ds(0, TAPS), :] = tail_in[p, :, strip_of(s)].astype(jnp.float32)
            total = direct[pl.ds(0, TAPS), lanes]
            for r in range(SUB):
                shifted = before[pl.ds(SUB - r, TAPS), :]
                for m in range(TAPS // SUB):
                    tap = long_ref[pl.ds(SUB * m + r, 1), lanes]
                    count = SUB * (m + 1)
                    head = total[:count] + tap * shifted[TAPS - count:]
                    total = jnp.concatenate((head, total[count:]), axis=0) if count < TAPS else head
            extend(lanes, (0,))
            gate = short(0, lanes, 0, rows)
            later = gate[TAPS:] * direct[pl.ds(TAPS, rows - TAPS), lanes]
            blocks[0, p, pl.ds(0, TAPS), strip_of(s)] = (gate[:TAPS] * total).astype(jnp.bfloat16)
            blocks[0, p, pl.ds(TAPS, rows - TAPS), strip_of(s)] = later.astype(jnp.bfloat16)
            return carry

        lax.fori_loop(0, strips, one, 0)
        send_own(1, p, ahead).start()
        send_own(2, p, behind).start()
        return carry

    lax.fori_loop(0, parts, gates, 0)

    own_columns.wait()
    columns.wait_recv()

    def tp_copy(slot):
        return pltpu.make_async_remote_copy(
            src_ref=sent.at[slot], dst_ref=other.at[slot], send_sem=tp_send.at[slot], recv_sem=tp_recv.at[slot],
            **peer(1 - t, cp),
        )

    def out_copy(slot):
        odd, step = slot % 2, (slot + 1) // 2
        return pltpu.make_async_remote_copy(
            src_ref=summed.at[slot], dst_ref=landed.at[my_piece], send_sem=out_send.at[slot],
            recv_sem=out_recv.at[my_piece], **peer(half_owner, cp_at(place + (1 - 2 * odd) * forth * step)),
        )

    width = weights.shape[2]
    tile = min(256, width)

    def bank(slot):
        return 2 if isinstance(slot, int) and slot == 0 else slot % 2

    def multiply(slot, p, first):
        depth_rows = pl.ds(pl.multiple_of(p * part, part), part)

        def one(j, carry):
            lanes = pl.ds(pl.multiple_of(j * tile, tile), tile)
            for side in range(2):
                value = jnp.dot(
                    blocks[slot, p], weights[side, depth_rows, lanes], preferred_element_type=jnp.float32
                )
                if not first:
                    value = value + totals[bank(slot), side, :, lanes]
                totals[bank(slot), side, :, lanes] = value
            return carry

        lax.fori_loop(0, width // tile, one, 0)

    def emit(slot):
        sent[slot] = totals[bank(slot), 1 - t].astype(jnp.bfloat16)
        tp_copy(slot).start()
        kept[slot] = totals[bank(slot), t].astype(jnp.bfloat16)

    def finish(slot):
        tp_copy(slot).wait_recv()
        total = (kept[slot].astype(jnp.float32) + other[slot].astype(jnp.float32)).astype(jnp.bfloat16)
        stays = jnp.logical_and(slot == 0, half_owner == t)

        @pl.when(stays)
        def _():
            landed[my_piece] = total

        @pl.when(jnp.logical_not(stays))
        def _():
            summed[slot] = total
            out_copy(slot).start()

    def receive(slot, p):
        pltpu.make_async_copy(blocks.at[slot, p], blocks.at[slot, p], block_recv.at[slot, p]).wait()

        onward = slot + 2 < n
        onward = jnp.logical_and(onward, jnp.logical_not(jnp.logical_and(slot == n - 3, takes_sixth)))
        onward = jnp.logical_and(onward, jnp.logical_not(jnp.logical_and(slot == n - 4, takes_seventh)))

        @pl.when(onward)
        def _():
            pass_on(slot, p).start()

        @pl.when(jnp.logical_and(slot == 2, takes_sixth))
        def _():
            chord(2, n - 1, p).start()

        @pl.when(jnp.logical_and(slot == 3, takes_seventh))
        def _():
            chord(3, n - 2, p).start()

    def take_last(p, first):
        pltpu.make_async_copy(blocks.at[n - 1, p], blocks.at[n - 1, p], block_recv.at[n - 1, p]).wait()
        multiply(n - 1, p, first)

    def both(i, p, first):
        odd, even = 2 * i - 1, 2 * i
        receive(odd, p)
        receive(even, p)
        if isinstance(i, int):
            multiply(0, p, first)
        multiply(odd, p, first)
        multiply(even, p, first)

    both(1, 0, True)
    lax.fori_loop(1, parts, lambda p, carry: (both(1, p, False), carry)[1], 0)
    for slot in range(3):
        emit(slot)

    def pair(i, carry):
        both(i, 0, True)

        @pl.when(i == 2)
        def _():
            finish(0)

        finish(2 * i - 2)
        finish(2 * i - 3)
        lax.fori_loop(1, parts, lambda p, carry: (both(i, p, False), carry)[1], 0)
        emit(2 * i - 1)
        emit(2 * i)
        return carry

    lax.fori_loop(2, depth, pair, 0)
    take_last(0, True)
    finish(n - 2)
    finish(n - 3)
    lax.fori_loop(1, parts, lambda p, carry: (take_last(p, False), carry)[1], 0)
    emit(n - 1)
    finish(n - 1)

    for piece in range(n):
        @pl.when(jnp.logical_not(jnp.logical_and(piece == my_piece, half_owner == t)))
        def _():
            pltpu.make_async_copy(landed.at[piece], landed.at[piece], out_recv.at[piece]).wait()

        out_ref[:, pl.ds(piece * width, width)] = landed[piece]

    columns.wait_send()

    @pl.when(jnp.logical_not(is_last))
    def _():
        edge_copy.wait_send()

    def drain_parts(p, carry):
        @pl.when(jnp.logical_not(is_last))
        def _():
            tail_copy(p).wait_send()

        send_own(1, p, ahead).wait_send()
        send_own(2, p, behind).wait_send()
        lax.fori_loop(1, n - 2, lambda slot, carry: (pass_on(slot, p).wait_send(), carry)[1], 0)
        return carry

    lax.fori_loop(0, parts, drain_parts, 0)

    def drain(slot, carry):
        tp_copy(slot).wait_send()

        @pl.when(jnp.logical_not(jnp.logical_and(slot == 0, half_owner == t)))
        def _():
            out_copy(slot).wait_send()

        return carry

    lax.fori_loop(0, n, drain, 0)


def mixer(features, short_filter, long_filter, skip_scale, out_weight, n):
    _, rows, channels = features.shape
    width = out_weight.shape[1]
    parts = 4
    part = channels // parts
    kind = jnp.bfloat16
    dma = pltpu.SemaphoreType.DMA
    whole = pl.BlockSpec(memory_space=pltpu.VMEM)
    return pl.pallas_call(
        functools.partial(mixer_kernel, n, parts),
        out_shape=jax.ShapeDtypeStruct((rows, n * width), kind),
        in_specs=[whole] * 4 + [pl.BlockSpec(memory_space=pl.ANY)],
        out_specs=whole,
        scratch_shapes=[
            pltpu.VMEM((n, parts, rows, part), kind),
            pltpu.VMEM((2, channels, width), kind),
            *[pltpu.VMEM((n, rows, width), kind)] * 5,
            pltpu.VMEM((3, 2, rows, width), jnp.float32),
            pltpu.VMEM((rows, channels), jnp.float32),
            *[pltpu.VMEM((2 * SUB, channels), kind)] * 2,
            *[pltpu.VMEM((parts, TAPS, part), kind)] * 2,
            pltpu.VMEM((3, SUB + rows, LANES), jnp.float32),
            pltpu.VMEM((SUB + rows, LANES), jnp.float32),
            pltpu.VMEM((TAPS + SUB, LANES), jnp.float32),
            dma, dma((2,)), dma((parts,)), dma((parts,)), dma((n, parts)), dma((n, parts)), dma, dma,
            dma((n,)), dma((n,)), dma((n,)), dma((n,)),
        ],
        compiler_params=pltpu.CompilerParams(
            collective_id=0, has_side_effects=True, vmem_limit_bytes=56 * 2**20
        ),
        cost_estimate=pl.CostEstimate(
            flops=4 * n * rows * channels * width, bytes_accessed=4 * channels * width, transcendentals=0
        ),
        name="mixer",
    )(features, short_filter, long_filter, skip_scale.reshape(1, channels), out_weight)


def local(on_ring, features, short_filter, long_filter, skip_scale, out_weight):
    rows = features.shape[1]
    if on_ring:
        return mixer(features, short_filter, long_filter, skip_scale, out_weight, lax.axis_size("cp") // 2)
    product, edge = halo_of(features, short_filter)
    halo = from_behind(product, "cp", 1)
    edge = from_behind(edge, "cp", 1)
    gated = gate_conv(features, halo, edge, short_filter, long_filter, skip_scale, rows)
    everyone = lax.all_gather(gated, "cp", axis=0, tiled=True)
    partial_value = jnp.dot(everyone, out_weight, preferred_element_type=jnp.float32).astype(jnp.bfloat16)
    mine = lax.all_to_all(partial_value, "cp", split_axis=0, concat_axis=1, tiled=True)
    return lax.psum_scatter(mine, "tp", scatter_dimension=1, tiled=True)


def solution(mesh):
    on_ring = mesh.shape["tp"] == 2 and mesh.shape["cp"] == 16
    return jax.shard_map(
        functools.partial(local, on_ring),
        mesh=mesh,
        in_specs=(P(None, "cp", "tp"), P(None, None, "tp"), P(None, "tp"), P("tp"), P("tp", "cp")),
        out_specs=P("cp", "tp"),
        check_vma=False,
    )
```

```python
import functools

import jax
import jax.numpy as jnp
from jax import lax
from jax.experimental import pallas as pl
from jax.experimental.pallas import tpu as pltpu
from jax.sharding import PartitionSpec as P

TAPS = 128
SHORT = 3
LANES = 128
SUB = 8


def from_behind(block, axis, distance):
    devices = range(lax.axis_size(axis))
    route = [(i - distance, i) for i in devices if i - distance in devices]
    return lax.ppermute(block, axis, route)


def conv_kernel(rows, width, feat_ref, halo_ref, edge_ref, short_ref, long_ref, skip_ref, out_ref, ext, prod):
    def strip(index, carry):
        lanes = pl.ds(pl.multiple_of(index * LANES, LANES), LANES)
        shorted = []
        for i in range(3):
            ext[i, pl.ds(0, SUB), :] = edge_ref[i, :, lanes].astype(jnp.float32)
            ext[i, pl.ds(SUB, rows), :] = feat_ref[i, :, lanes].astype(jnp.float32)
            total = short_ref[i, pl.ds(0, 1), lanes] * ext[i, pl.ds(SUB, rows), :]
            for lag in range(1, SHORT):
                total = total + short_ref[i, pl.ds(lag, 1), lanes] * ext[i, pl.ds(SUB - lag, rows), :]
            shorted.append(total)
        product = shorted[1] * shorted[2]
        prod[pl.ds(0, TAPS), :] = halo_ref[:, lanes].astype(jnp.float32)
        prod[pl.ds(TAPS, rows), :] = product
        total = skip_ref[:, lanes] * product
        span = rows + TAPS - SUB
        for r in range(SUB):
            shifted = prod[pl.ds(SUB - r, span), :]
            for m in range(TAPS // SUB):
                begin = TAPS - SUB - SUB * m
                total = total + long_ref[pl.ds(SUB * m + r, 1), lanes] * shifted[begin:begin + rows]
        out_ref[pl.ds(0, rows), lanes] = (shorted[0] * total).astype(jnp.bfloat16)
        if out_ref.shape[0] > rows:
            out_ref[pl.ds(rows, out_ref.shape[0] - rows), lanes] = jnp.zeros(
                (out_ref.shape[0] - rows, LANES), jnp.bfloat16
            )
        return carry

    lax.fori_loop(0, width // LANES, strip, 0)


def gate_conv(features, halo, edge, short_filter, long_filter, skip_scale, out_rows):
    _, rows, channels = features.shape
    width = min(512, channels)
    return pl.pallas_call(
        functools.partial(conv_kernel, rows, width),
        grid=(channels // width,),
        out_shape=jax.ShapeDtypeStruct((out_rows, channels), jnp.bfloat16),
        in_specs=[
            pl.BlockSpec((3, rows, width), lambda c: (0, 0, c)),
            pl.BlockSpec((TAPS, width), lambda c: (0, c)),
            pl.BlockSpec((3, SUB, width), lambda c: (0, 0, c)),
            pl.BlockSpec((3, SHORT, width), lambda c: (0, 0, c)),
            pl.BlockSpec((TAPS, width), lambda c: (0, c)),
            pl.BlockSpec((1, width), lambda c: (0, c)),
        ],
        out_specs=pl.BlockSpec((out_rows, width), lambda c: (0, c)),
        scratch_shapes=[
            pltpu.VMEM((3, SUB + rows, LANES), jnp.float32),
            pltpu.VMEM((TAPS + rows, LANES), jnp.float32),
        ],
        compiler_params=pltpu.CompilerParams(vmem_limit_bytes=32 * 2**20),
        cost_estimate=pl.CostEstimate(
            flops=2 * TAPS * rows * channels, bytes_accessed=10 * rows * channels, transcendentals=0
        ),
        name="gate_conv",
    )(features, halo, edge, short_filter, long_filter, skip_scale.reshape(1, channels))


def halo_of(features, short_filter):
    rows = features.shape[1]
    tail = features[1:, rows - TAPS - SHORT + 1:, :].astype(jnp.float32)
    shorted = sum(
        short_filter[1:, lag, None, :] * tail[:, SHORT - 1 - lag:SHORT - 1 - lag + TAPS] for lag in range(SHORT)
    )
    product = (shorted[0] * shorted[1]).astype(jnp.bfloat16)
    return product, features[:, rows - SUB:, :]


def mixer_kernel(
    n, parts, feat_ref, short_ref, long_ref, skip_ref, weight_ref, out_ref,
    blocks, weights, kept, sent, other, summed, landed, totals, direct, edge_out, edge_in, tail_out, tail_in, ext, prod, before,
    own_sem, edge_sem, tail_send, tail_recv, block_send, block_recv, weight_send, weight_recv,
    tp_send, tp_recv, out_send, out_recv,
):
    t, cp = lax.axis_index("tp"), lax.axis_index("cp")
    rows = feat_ref.shape[1]
    part = blocks.shape[3]
    core, chip = cp % 2, cp // 2
    x, z = chip % 2, chip // 2
    depth = n // 2
    place = x * (n - 1 - z) + (1 - x) * z
    forth = 1 - 2 * core
    half_owner = chip // depth
    my_piece = (chip % depth) * 2 + t

    def cp_at(ring_place):
        r = (ring_place + 2 * n) % n
        rx = r // depth
        rz = rx * (n - 1 - r) + (1 - rx) * r
        return (rz * 2 + rx) * 2 + core

    def peer(a, b):
        return dict(device_id=(a, b), device_id_type=pl.DeviceIdType.MESH)

    ahead, behind = cp_at(place + forth), cp_at(place - forth)
    sibling = cp + 1 - 2 * core
    across = cp_at(n - 1 - place)
    takes_seventh, takes_sixth = place % depth == 2 - core, place % depth == 1 + core
    is_first, is_last = cp == 0, cp == 2 * n - 1

    barrier = pltpu.get_barrier_semaphore()
    for device in ((t, ahead), (t, behind), (t, sibling), (1 - t, cp)):
        pl.semaphore_signal(barrier, inc=1, **peer(*device))

    @pl.when(jnp.logical_or(takes_seventh, takes_sixth))
    def _():
        pl.semaphore_signal(barrier, inc=1, **peer(t, across))

    @pl.when(cp > 0)
    def _():
        pl.semaphore_signal(barrier, inc=1, **peer(t, cp - 1))

    def greet(i, carry):
        sender = (t * depth + i // 2) * 2 + core

        @pl.when(jnp.logical_or(i % 2 != t, sender != cp))
        def _():
            pl.semaphore_signal(barrier, inc=1, **peer(i % 2, sender))

        return carry

    lax.fori_loop(0, n, greet, 0)
    has_chord, has_next = (place % depth + 1) // 2 % 2, (4 * n - 3 - cp) // (2 * n - 1)

    columns = pltpu.make_async_remote_copy(
        src_ref=weight_ref, dst_ref=weights.at[core], send_sem=weight_send, recv_sem=weight_recv, **peer(t, sibling)
    )
    own_columns = pltpu.make_async_copy(weight_ref, weights.at[core], own_sem)
    edge_copy = pltpu.make_async_remote_copy(
        src_ref=edge_out, dst_ref=edge_in, send_sem=edge_sem.at[0], recv_sem=edge_sem.at[1], **peer(t, cp + 1)
    )

    def tail_copy(p):
        return pltpu.make_async_remote_copy(
            src_ref=tail_out.at[p], dst_ref=tail_in.at[p], send_sem=tail_send.at[p], recv_sem=tail_recv.at[p],
            **peer(t, cp + 1),
        )

    def strip_of(index):
        return pl.ds(pl.multiple_of(index * LANES, LANES), LANES)

    strips = part // LANES

    def edges(index, carry):
        lanes = strip_of(index)
        q, k, v = (feat_ref[i, pl.ds(rows - SUB, SUB), lanes].astype(jnp.float32) for i in range(3))
        row = lax.broadcasted_iota(jnp.int32, (SUB, LANES), 0)
        kv = jnp.where(row >= SUB - 2, k, pltpu.roll(v, SUB - 2, 0))
        edge_out[:, lanes] = jnp.concatenate((q, kv), axis=0).astype(jnp.bfloat16)
        return carry

    lax.fori_loop(0, parts * strips, edges, 0)

    def short(i, lanes, begin, count):
        total = short_ref[i, pl.ds(0, 1), lanes] * ext[i, pl.ds(SUB + begin, count), :]
        for lag in range(1, SHORT):
            total = total + short_ref[i, pl.ds(lag, 1), lanes] * ext[i, pl.ds(SUB + begin - lag, count), :]
        return total

    def tails(p):
        def one(s, carry):
            lanes = strip_of(p * strips + s)
            for i in (1, 2):
                ext[i, pl.ds(SUB, rows), :] = feat_ref[i, :, lanes].astype(jnp.float32)
            product = short(1, lanes, rows - TAPS, TAPS) * short(2, lanes, rows - TAPS, TAPS)
            tail_out[p, :, strip_of(s)] = product.astype(jnp.bfloat16)
            return carry

        lax.fori_loop(0, strips, one, 0)

    def send_tail(p):
        @pl.when(jnp.logical_not(is_last))
        def _():
            tail_copy(p).start()

    tails(0)
    pl.semaphore_wait(barrier, 4 + n - 1 + (half_owner + t) % 2 + has_chord + has_next)

    @pl.when(jnp.logical_not(is_last))
    def _():
        edge_copy.start()

    send_tail(0)
    own_columns.start()
    lax.fori_loop(1, parts, lambda p, carry: (tails(p), send_tail(p), carry)[2], 0)
    columns.start()

    @pl.when(is_first)
    def _():
        edge_in[...] = jnp.zeros_like(edge_in)
        tail_in[...] = jnp.zeros_like(tail_in)

    @pl.when(jnp.logical_not(is_first))
    def _():
        edge_copy.wait_recv()

    def extend(lanes, which):
        edge = edge_in[:, lanes].astype(jnp.float32)
        q, kv = edge[:SUB], edge[SUB:]
        ahead_rows = (q, kv, pltpu.roll(kv, 2, 0))
        for i in which:
            ext[i, pl.ds(0, SUB), :] = ahead_rows[i]
            ext[i, pl.ds(SUB, rows), :] = feat_ref[i, :, lanes].astype(jnp.float32)

    prod[pl.ds(0, SUB), :] = jnp.zeros((SUB, LANES), jnp.float32)

    def own_strip(index, carry):
        lanes = strip_of(index)
        extend(lanes, (1, 2))
        product = short(1, lanes, 0, rows) * short(2, lanes, 0, rows)
        prod[pl.ds(SUB, rows), :] = product
        total = skip_ref[:, lanes] * product
        for r in range(SUB):
            shifted = prod[pl.ds(SUB - r, rows), :]
            for m in range(TAPS // SUB):
                tap = long_ref[pl.ds(SUB * m + r, 1), lanes]
                rest = total[SUB * m:] + tap * shifted[:rows - SUB * m]
                total = jnp.concatenate((total[:SUB * m], rest), axis=0) if m else rest
        direct[:, lanes] = total
        return carry

    def own_rows(p):
        lax.fori_loop(p * strips, (p + 1) * strips, own_strip, 0)

    def send_own(slot, p, device):
        return pltpu.make_async_remote_copy(
            src_ref=blocks.at[0, p], dst_ref=blocks.at[slot, p], send_sem=block_send.at[slot, p],
            recv_sem=block_recv.at[slot, p], **peer(t, device),
        )

    def pass_on(slot, p):
        odd = slot % 2
        return pltpu.make_async_remote_copy(
            src_ref=blocks.at[slot, p], dst_ref=blocks.at[slot + 2, p], send_sem=block_send.at[slot + 2, p],
            recv_sem=block_recv.at[slot + 2, p], **peer(t, odd * ahead + (1 - odd) * behind),
        )

    def chord(source, slot, p):
        return pltpu.make_async_remote_copy(
            src_ref=blocks.at[source, p], dst_ref=blocks.at[slot, p], send_sem=block_send.at[slot, p],
            recv_sem=block_recv.at[slot, p], **peer(t, across),
        )

    before[pl.ds(TAPS, SUB), :] = jnp.zeros((SUB, LANES), jnp.float32)

    def gates(p, carry):
        @pl.when(p + 1 < parts)
        def _():
            own_rows(p + 1)

        @pl.when(jnp.logical_not(is_first))
        def _():
            tail_copy(p).wait_recv()

        def one(s, carry):
            lanes = strip_of(p * strips + s)
            before[pl.ds(0, TAPS), :] = tail_in[p, :, strip_of(s)].astype(jnp.float32)
            total = direct[pl.ds(0, TAPS), lanes]
            for r in range(SUB):
                shifted = before[pl.ds(SUB - r, TAPS), :]
                for m in range(TAPS // SUB):
                    tap = long_ref[pl.ds(SUB * m + r, 1), lanes]
                    count = SUB * (m + 1)
                    head = total[:count] + tap * shifted[TAPS - count:]
                    total = jnp.concatenate((head, total[count:]), axis=0) if count < TAPS else head
            extend(lanes, (0,))
            gate = short(0, lanes, 0, rows)
            later = gate[TAPS:] * direct[pl.ds(TAPS, rows - TAPS), lanes]
            blocks[0, p, pl.ds(0, TAPS), strip_of(s)] = (gate[:TAPS] * total).astype(jnp.bfloat16)
            blocks[0, p, pl.ds(TAPS, rows - TAPS), strip_of(s)] = later.astype(jnp.bfloat16)
            return carry

        lax.fori_loop(0, strips, one, 0)
        send_own(1, p, ahead).start()
        send_own(2, p, behind).start()
        return carry

    own_rows(0)
    lax.fori_loop(0, parts, gates, 0)

    own_columns.wait()
    columns.wait_recv()

    def tp_copy(slot):
        return pltpu.make_async_remote_copy(
            src_ref=sent.at[slot], dst_ref=other.at[slot], send_sem=tp_send.at[slot], recv_sem=tp_recv.at[slot],
            **peer(1 - t, cp),
        )

    def out_copy(slot):
        odd, step = slot % 2, (slot + 1) // 2
        return pltpu.make_async_remote_copy(
            src_ref=summed.at[slot], dst_ref=landed.at[my_piece], send_sem=out_send.at[slot],
            recv_sem=out_recv.at[my_piece], **peer(half_owner, cp_at(place + (1 - 2 * odd) * forth * step)),
        )

    width = weights.shape[2]
    tile = min(256, width)

    def multiply(slot, p, first):
        depth_rows = pl.ds(pl.multiple_of(p * part, part), part)

        def one(j, carry):
            lanes = pl.ds(pl.multiple_of(j * tile, tile), tile)
            for side in range(2):
                value = jnp.dot(
                    blocks[slot, p], weights[side, depth_rows, lanes], preferred_element_type=jnp.float32
                )
                if not first:
                    value = value + totals[slot % 2, side, :, lanes]
                totals[slot % 2, side, :, lanes] = value
            return carry

        lax.fori_loop(0, width // tile, one, 0)

    def emit(slot):
        sent[slot] = totals[slot % 2, 1 - t].astype(jnp.bfloat16)
        tp_copy(slot).start()
        kept[slot] = totals[slot % 2, t].astype(jnp.bfloat16)

    def finish(slot):
        tp_copy(slot).wait_recv()
        total = (kept[slot].astype(jnp.float32) + other[slot].astype(jnp.float32)).astype(jnp.bfloat16)
        stays = jnp.logical_and(slot == 0, half_owner == t)

        @pl.when(stays)
        def _():
            landed[my_piece] = total

        @pl.when(jnp.logical_not(stays))
        def _():
            summed[slot] = total
            out_copy(slot).start()

    def take(slot, p, first):
        pltpu.make_async_copy(blocks.at[slot, p], blocks.at[slot, p], block_recv.at[slot, p]).wait()

        onward = slot + 2 < n
        onward = jnp.logical_and(onward, jnp.logical_not(jnp.logical_and(slot == n - 3, takes_sixth)))
        onward = jnp.logical_and(onward, jnp.logical_not(jnp.logical_and(slot == n - 4, takes_seventh)))

        @pl.when(onward)
        def _():
            pass_on(slot, p).start()

        @pl.when(jnp.logical_and(slot == 2, takes_sixth))
        def _():
            chord(2, n - 1, p).start()

        @pl.when(jnp.logical_and(slot == 3, takes_seventh))
        def _():
            chord(3, n - 2, p).start()

        multiply(slot, p, first)

    def take_last(p, first):
        pltpu.make_async_copy(blocks.at[n - 1, p], blocks.at[n - 1, p], block_recv.at[n - 1, p]).wait()
        multiply(n - 1, p, first)

    multiply(0, 0, True)
    lax.fori_loop(1, parts, lambda p, carry: (multiply(0, p, False), carry)[1], 0)
    emit(0)

    def pair(i, carry):
        odd, even = 2 * i - 1, 2 * i

        def both(p, first):
            take(odd, p, first)
            take(even, p, first)

        both(0, True)
        finish(odd - 1)

        @pl.when(i > 1)
        def _():
            finish(odd - 2)

        lax.fori_loop(1, parts, lambda p, carry: (both(p, False), carry)[1], 0)
        emit(odd)
        emit(even)
        return carry

    lax.fori_loop(1, depth, pair, 0)
    take_last(0, True)
    finish(n - 2)
    finish(n - 3)
    lax.fori_loop(1, parts, lambda p, carry: (take_last(p, False), carry)[1], 0)
    emit(n - 1)
    finish(n - 1)

    for piece in range(n):
        @pl.when(jnp.logical_not(jnp.logical_and(piece == my_piece, half_owner == t)))
        def _():
            pltpu.make_async_copy(landed.at[piece], landed.at[piece], out_recv.at[piece]).wait()

        out_ref[:, pl.ds(piece * width, width)] = landed[piece]

    columns.wait_send()

    @pl.when(jnp.logical_not(is_last))
    def _():
        edge_copy.wait_send()

    def drain_parts(p, carry):
        @pl.when(jnp.logical_not(is_last))
        def _():
            tail_copy(p).wait_send()

        send_own(1, p, ahead).wait_send()
        send_own(2, p, behind).wait_send()
        lax.fori_loop(1, n - 2, lambda slot, carry: (pass_on(slot, p).wait_send(), carry)[1], 0)
        return carry

    lax.fori_loop(0, parts, drain_parts, 0)

    def drain(slot, carry):
        tp_copy(slot).wait_send()

        @pl.when(jnp.logical_not(jnp.logical_and(slot == 0, half_owner == t)))
        def _():
            out_copy(slot).wait_send()

        return carry

    lax.fori_loop(0, n, drain, 0)


def mixer(features, short_filter, long_filter, skip_scale, out_weight, n):
    _, rows, channels = features.shape
    width = out_weight.shape[1]
    parts = 4
    part = channels // parts
    kind = jnp.bfloat16
    dma = pltpu.SemaphoreType.DMA
    whole = pl.BlockSpec(memory_space=pltpu.VMEM)
    return pl.pallas_call(
        functools.partial(mixer_kernel, n, parts),
        out_shape=jax.ShapeDtypeStruct((rows, n * width), kind),
        in_specs=[whole] * 4 + [pl.BlockSpec(memory_space=pl.ANY)],
        out_specs=whole,
        scratch_shapes=[
            pltpu.VMEM((n, parts, rows, part), kind),
            pltpu.VMEM((2, channels, width), kind),
            *[pltpu.VMEM((n, rows, width), kind)] * 5,
            pltpu.VMEM((2, 2, rows, width), jnp.float32),
            pltpu.VMEM((rows, channels), jnp.float32),
            *[pltpu.VMEM((2 * SUB, channels), kind)] * 2,
            *[pltpu.VMEM((parts, TAPS, part), kind)] * 2,
            pltpu.VMEM((3, SUB + rows, LANES), jnp.float32),
            pltpu.VMEM((SUB + rows, LANES), jnp.float32),
            pltpu.VMEM((TAPS + SUB, LANES), jnp.float32),
            dma, dma((2,)), dma((parts,)), dma((parts,)), dma((n, parts)), dma((n, parts)), dma, dma,
            dma((n,)), dma((n,)), dma((n,)), dma((n,)),
        ],
        compiler_params=pltpu.CompilerParams(
            collective_id=0, has_side_effects=True, vmem_limit_bytes=56 * 2**20
        ),
        cost_estimate=pl.CostEstimate(
            flops=4 * n * rows * channels * width, bytes_accessed=4 * channels * width, transcendentals=0
        ),
        name="mixer",
    )(features, short_filter, long_filter, skip_scale.reshape(1, channels), out_weight)


def local(on_ring, features, short_filter, long_filter, skip_scale, out_weight):
    rows = features.shape[1]
    if on_ring:
        return mixer(features, short_filter, long_filter, skip_scale, out_weight, lax.axis_size("cp") // 2)
    product, edge = halo_of(features, short_filter)
    halo = from_behind(product, "cp", 1)
    edge = from_behind(edge, "cp", 1)
    gated = gate_conv(features, halo, edge, short_filter, long_filter, skip_scale, rows)
    everyone = lax.all_gather(gated, "cp", axis=0, tiled=True)
    partial_value = jnp.dot(everyone, out_weight, preferred_element_type=jnp.float32).astype(jnp.bfloat16)
    mine = lax.all_to_all(partial_value, "cp", split_axis=0, concat_axis=1, tiled=True)
    return lax.psum_scatter(mine, "tp", scatter_dimension=1, tiled=True)


def solution(mesh):
    on_ring = mesh.shape["tp"] == 2 and mesh.shape["cp"] == 16
    return jax.shard_map(
        functools.partial(local, on_ring),
        mesh=mesh,
        in_specs=(P(None, "cp", "tp"), P(None, None, "tp"), P(None, "tp"), P("tp"), P("tp", "cp")),
        out_specs=P("cp", "tp"),
        check_vma=False,
    )
```
